256 devices in a mesh: dom: 128 (over x, z, y), fn: 2 (over core).
Axes of the slice: x: 4, y: 4, z: 8, core: 2. Of those that a mesh axis runs over, the one named last changes fastest.
Arguments:
- rhs: float32 [6144, 16, 320], P('dom', 'fn'), may hold values from -6 to 6
- dinv: bfloat16 [6144, 320, 320], P('dom')
- extract: float32 [6, 320, 80], replicated, may hold values from -0.3125 to 0.3125
- lift: float32 [6, 80, 320], replicated, may hold values from -0.625 to 0.625
- coef: float32 [6144, 6], P('dom'), may hold values from 0.1 to 0.45
- nbr: int32 [6144, 6], P('dom'), may hold values from -1 to 63, as said below
- colour: int32 [6144], P('dom'), may hold values from 0 to 1
- counts: int32 [128], P('dom'), may hold values from 1 to 48, as said below
- send_lo: int32 [1024], P('dom'), may hold values from 0 to 47, as said below
- send_hi: int32 [1024], P('dom'), may hold values from 0 to 47, as said below
- rec_elem: int32 [16384], P('dom'), may hold values from 0 to 47, as said below
- rec_owner: int32 [16384, 1], P('dom'), may hold values from 0 to 127; in each aligned block of 128 rows (0 to 127, 128 to 255, ...) at most 2 rows name the same one
- rec_box: int32 [16384], P('dom'), may hold values from 0 to 3
- rec_weight: float32 [16384], P('dom'), may hold values from 0.3 to 3
- wall_map: bfloat16 [320, 128], replicated, may hold values from -0.3125 to 0.3125
- fweights: float32 [16], P('fn'), may hold values from -1.5 to 1.5
Outputs:
- grad: float32 [512, 16, 128], P('dom', 'fn')
- combined: float32 [512, 128], P('dom')
The draws below stay inside these ranges and needn't reach their ends.
Inputs may be any that keep to these rules, and one draw needn't show every extreme that they name: `counts`: each count is at least 1, and some partition is full (48) in every draw. `nbr`: codes of a live element: -1 a wall, below 48 a live element of the same partition, 48 + s import slot s below (face 0 only), 56 + s import slot s above (face 1 only). `send_lo`: live elements of the sending partition. `send_hi`: live elements of the sending partition. `rec_elem`: live elements of the record's partition. `rec_owner`: the records of one partition name one owner at most 2 times.
All inputs are finite; a program needn't handle non-finite values.
Results may differ from the reference program's by a relative error of at most 0.0034.
Values sent between devices are 32-bit elements; how exact they have to be, the bound alone decides.
A program may use at most 64 MiB of HBM per device.

```python
import math
import jax
import jax.numpy as jnp
import numpy as np
from jax import lax

NB = 320
NT = 80
FUNCS = 16
WALL = 128
E_DEV = 48
S = 8
BOX_DEV = 4
CAP = 2
SWEEPS = 2
SURF_DEV = 128
ELEMS = 6144
RECS = 16384
N_DOM = 128


def shared_layout(key):
    key_count, key_pick = jax.random.split(key)
    counts = jax.random.randint(key_count, (N_DOM,), max(E_DEV // 2, 1), E_DEV + 1)
    pick = jax.random.randint(key_pick, (), 0, N_DOM)
    return jnp.where(jnp.arange(N_DOM) == pick, E_DEV, counts).astype(jnp.int32)


def draw_counts(key, part):
    counts = shared_layout(key)
    return counts


def draw_send_lo(key, part):
    counts = shared_layout(key)
    key = jax.random.fold_in(key, 11)
    raw = jax.random.randint(key, (N_DOM, S), 0, 1 << 20)
    return (raw % counts[:, None]).reshape(-1).astype(jnp.int32)


def draw_send_hi(key, part):
    counts = shared_layout(key)
    key = jax.random.fold_in(key, 12)
    raw = jax.random.randint(key, (N_DOM, S), 0, 1 << 20)
    return (raw % counts[:, None]).reshape(-1).astype(jnp.int32)


def draw_rec_elem(key, part):
    counts = shared_layout(key)
    key = jax.random.fold_in(key, 14)
    raw = jax.random.randint(key, (N_DOM, SURF_DEV), 0, 1 << 20)
    return (raw % counts[:, None]).reshape(-1).astype(jnp.int32)


def draw_nbr(key, part):
    counts = shared_layout(key)
    key = jax.random.fold_in(key, 13)
    key_local, key_kind, key_slot = jax.random.split(key, 3)
    raw = jax.random.randint(key_local, (N_DOM, E_DEV, 6), 0, 1 << 20)
    local = raw % counts[:, None, None]
    kind = jax.random.randint(key_kind, (N_DOM, E_DEV, 6), 0, 4)
    slot = jax.random.randint(key_slot, (N_DOM, E_DEV, 6), 0, S)
    face = jnp.arange(6)[None, None, :]
    below = (face == 0) & (kind < 2)
    above = (face == 1) & (kind < 2)
    wall = (face >= 2) & (kind == 0)
    code = jnp.where(below, E_DEV + slot, jnp.where(above, E_DEV + S + slot, jnp.where(wall, -1, local)))
    return code.reshape(N_DOM * E_DEV, 6).astype(jnp.int32)


def draw_dinv(key, part):
    key = jax.random.fold_in(key, 15)
    key_diag, key_off = jax.random.split(key)
    diag = jax.random.uniform(key_diag, (N_DOM * E_DEV, 1, 1), jnp.float32, 0.5, 1.0)
    off = jax.random.normal(key_off, (N_DOM * E_DEV, NB, NB), jnp.float32) * (0.6 / NB ** 0.5)
    return (diag * jnp.eye(NB, dtype=jnp.float32)[None] + off).astype(jnp.bfloat16)


def place_ends(entries, rng, smallest, high):
    extent = entries.shape
    index_at = [jax.random.randint(jax.random.fold_in(rng, axis), (), 0, extent[axis]) for axis in range(len(extent))]
    entries = entries.at[tuple(index_at)].set(smallest)
    longest = extent.index(max(extent))
    index_at[longest] = (index_at[longest] + 1) % extent[longest]
    return entries.at[tuple(index_at)].set(high)


def levels(own_key, extent, cuts, smallest, largest):
    gain = 1.0
    for position, blocks in cuts:
        heights = jax.random.uniform(jax.random.fold_in(jax.random.fold_in(own_key, 6), position), (blocks,), jnp.float32, smallest / len(cuts), largest / len(cuts))
        gain = gain * jnp.repeat(jnp.exp(heights), extent[position] // blocks).reshape((-1,) + (1,) * (len(extent) - 1 - position))
    return gain


def routed_block(stream_key, own, number, rows, number_of, top, most, skew):
    order = jax.random.permutation(stream_key, number_of)
    heavy_load, ordinary = shares(number_of, rows * top, most, skew, True), shares(number_of, rows * top, most, skew, False)
    places = jnp.arange(number_of)

    def named(tallies, turn):
        used = int((tallies > 0).sum())
        fixed = max(1, used // 4)
        passed = fixed + (places - fixed + turn * (used - fixed)) % max(1, number_of - fixed)
        return jnp.zeros((number_of,), jnp.int32).at[order[jnp.where(places < fixed, places, passed)]].set(jnp.asarray(tallies, jnp.int32))

    tallies = jnp.where(number % 4 == 0, named(heavy_load, number // 4), named(ordinary, number - number // 4 - 1))
    mixed = jax.random.permutation(jax.random.fold_in(own, 3), number_of)
    source_of, sink = mixed[0:number_of // 2 * 2:2], mixed[1:number_of // 2 * 2:2]
    margin = jnp.minimum(tallies[source_of] - 1, most - tallies[sink]) // 2
    margin = jnp.where((source_of == order[0]) | (sink == order[0]) | (tallies[sink] == 0), 0, jnp.maximum(margin, 0))
    passed = jax.random.randint(jax.random.fold_in(own, 4), (number_of // 2,), 0, 1 << 20) % (margin + 1)
    tallies = tallies.at[source_of].add(-passed).at[sink].add(passed)
    members = jnp.searchsorted(jnp.cumsum(tallies), jnp.arange(rows * top), side="right").astype(jnp.int32)
    grid = members.reshape(top, rows).T
    grid = grid[jax.random.permutation(jax.random.fold_in(own, 1), rows)]
    turn = jax.random.randint(jax.random.fold_in(own, 2), (rows, 1), 0, top)
    return jnp.take_along_axis(grid, (jnp.arange(top)[None, :] + turn) % top, axis=1)


def shares(number_of, total, limit, skew, full):
    portions = [(1 << 20) // math.isqrt(grade ** skew) + 1 for grade in range(1, number_of + 1)]
    largest = limit if full else min(limit, max(-(-total // number_of), total * portions[0] // sum(portions)))
    least = 1 if total - largest >= number_of - 1 else 0
    given, surplus = [largest] + [least] * (number_of - 1), total - largest - least * (number_of - 1)
    while surplus > 0:
        candidates = [i for i in range(1, number_of) if given[i] < largest] or [i for i in range(1, number_of) if given[i] < limit]
        mass, remaining = sum([portions[i] for i in candidates]), surplus
        for i in candidates:
            more = min(limit - given[i], max(1, remaining * portions[i] // mass), surplus)
            given[i] = given[i] + more
            surplus = surplus - more
    return np.array(given)


def gaussian(own_key, dims, scale, most, shards=(), kind=jnp.bfloat16):
    loudness = levels(own_key, dims, shards, -0.22, 0.18) if shards else 1.0
    entries = jax.random.normal(own_key, dims, jnp.float32) * scale * loudness
    return jnp.minimum(jnp.maximum(entries, -most), most).astype(kind)


def setup_inputs(seed: int = 0) -> dict:
    key_list = jax.random.split(jax.random.key(seed), 17)
    rhs = gaussian(key_list[0], (ELEMS, FUNCS, NB), 1.0, 6.0, ((0, 128), (1, 2)), jnp.float32)
    dinv = draw_dinv(jax.random.fold_in(key_list[16], 71), 0)
    extract = gaussian(key_list[2], (6, NB, NT), NB ** -0.5, 0.3125, (), jnp.float32)
    lift = gaussian(key_list[3], (6, NT, NB), NT ** -0.5, 0.625, (), jnp.float32)
    coef = jnp.clip(0.1 + 0.35 * jax.random.uniform(key_list[4], (ELEMS, 6), jnp.float32) ** levels(key_list[4], (ELEMS, 6), ((0, 128),), -0.2, 0.2), 0.1, 0.45)
    nbr = draw_nbr(jax.random.fold_in(key_list[16], 71), 0)
    colour = place_ends(jax.random.randint(key_list[6], (ELEMS,), 0, 2), jax.random.fold_in(key_list[6], 1), 0, 1).astype(jnp.int32)
    counts = draw_counts(jax.random.fold_in(key_list[16], 71), 0)
    send_lo = draw_send_lo(jax.random.fold_in(key_list[16], 71), 0)
    send_hi = draw_send_hi(jax.random.fold_in(key_list[16], 71), 0)
    rec_elem = draw_rec_elem(jax.random.fold_in(key_list[16], 71), 0)
    rec_owner_keys = jax.random.split(jax.random.fold_in(key_list[11], 1), RECS // SURF_DEV)
    rec_owner_turns = jax.random.permutation(jax.random.fold_in(key_list[11], 3), RECS // SURF_DEV)
    rec_owner = jax.vmap(lambda own, number: routed_block(jax.random.fold_in(key_list[11], 2), own, number, SURF_DEV, N_DOM, 1, CAP, 2))(rec_owner_keys, rec_owner_turns).reshape((RECS, 1))
    rec_box = place_ends(jax.random.randint(key_list[12], (RECS,), 0, BOX_DEV), jax.random.fold_in(key_list[12], 1), 0, BOX_DEV - 1).astype(jnp.int32)
    rec_weight = jnp.clip(jnp.exp(math.log(3.0) - 2.3025851 * jax.random.uniform(key_list[13], (RECS,), jnp.float32) ** levels(key_list[13], (RECS,), ((0, 128),), -0.2, 0.2)), 0.3, 3.0)
    wall_map = gaussian(key_list[14], (NB, WALL), NB ** -0.5, 0.3125)
    fweights = jnp.clip(jax.random.uniform(key_list[15], (FUNCS,), jnp.float32, -1.5, 1.5) * levels(key_list[15], (FUNCS,), ((0, 2),), -0.4, 0.0), -1.5, 1.5)
    return {"rhs": rhs, "dinv": dinv, "extract": extract, "lift": lift, "coef": coef, "nbr": nbr, "colour": colour, "counts": counts, "send_lo": send_lo, "send_hi": send_hi, "rec_elem": rec_elem, "rec_owner": rec_owner, "rec_box": rec_box, "rec_weight": rec_weight, "wall_map": wall_map, "fweights": fweights}


HIGH = lax.Precision.HIGHEST


def reference(rhs, dinv, extract, lift, coef, nbr, colour, counts, send_lo, send_hi, rec_elem, rec_owner, rec_box, rec_weight, wall_map, fweights):
    parts = N_DOM
    slots = E_DEV
    rhs4 = rhs.reshape(parts, slots, FUNCS, NB)
    dinv4 = dinv.reshape(parts, slots, NB, NB).astype(jnp.float32)
    coef3 = coef.reshape(parts, slots, 6)
    nbr3 = nbr.reshape(parts, slots, 6)
    colour2 = colour.reshape(parts, slots)
    live = jnp.arange(slots, dtype=jnp.int32)[None, :] < counts[:, None]
    opposite = jnp.array([1, 0, 3, 2, 5, 4], dtype=jnp.int32)
    index = jnp.where(nbr3 < 0, slots * 6 + 2 * S,
                      jnp.where(nbr3 < slots, nbr3 * 6 + opposite[None, None, :], slots * 6 + nbr3 - slots)).astype(jnp.int32)
    index = index.reshape(parts, slots * 6)
    lower_list = send_lo.reshape(parts, S)
    upper_list = send_hi.reshape(parts, S)
    devices = jnp.arange(parts, dtype=jnp.int32)[:, None]
    psi = jnp.zeros((parts, slots, FUNCS, NB), jnp.float32)
    for sweep in range(SWEEPS):
        for shade in range(2):
            traces = jnp.einsum('dekn,gnt->degkt', psi, extract, precision=HIGH)
            out_upper = traces[devices, upper_list, 1]
            out_lower = traces[devices, lower_list, 0]
            from_below = jnp.roll(out_upper, 1, axis=0)
            from_above = jnp.roll(out_lower, -1, axis=0)
            table = jnp.concatenate([traces.reshape(parts, slots * 6, FUNCS, NT), from_below, from_above,
                                     jnp.zeros((parts, 1, FUNCS, NT), jnp.float32)], axis=1)
            near = jnp.take_along_axis(table, index[:, :, None, None], axis=1).reshape(parts, slots, 6, FUNCS, NT)
            near = near * coef3[:, :, :, None, None]
            contrib = jnp.einsum('defkt,ftn->dekn', near, lift, precision=HIGH)
            resid = (rhs4 - contrib).astype(jnp.bfloat16)
            resid = lax.optimization_barrier(resid).astype(jnp.float32)
            fresh = jnp.einsum('dekn,denm->dekm', resid, dinv4, precision=HIGH)
            mask = (colour2 == shade) & live
            psi = jnp.where(mask[:, :, None, None], fresh, psi)
    picked = psi[devices, rec_elem.reshape(parts, SURF_DEV)]
    vals = jnp.einsum('dskn,nw->dskw', picked, wall_map.astype(jnp.float32), precision=HIGH)
    vals = vals * rec_weight.reshape(parts, SURF_DEV)[:, :, None, None]
    target = (rec_owner[:, 0] * BOX_DEV + rec_box).astype(jnp.int32)
    grad = jax.ops.segment_sum(vals.reshape(parts * SURF_DEV, FUNCS, WALL), target, num_segments=BOX_DEV * parts)
    combined = jnp.einsum('bjw,j->bw', grad, fweights, precision=HIGH)
    return grad, combined
```

```python
import functools
import jax
import jax.numpy as jnp
from jax import lax
from jax.experimental import pallas as pl
from jax.experimental.pallas import tpu as pltpu
from jax.sharding import PartitionSpec as P

BOX_DEV = 4
SWEEPS = 2
OPPOSITE = (1, 0, 3, 2, 5, 4)
LANES = 128
GRIDS = {128: (4, 8, 4), 8: (2, 2, 2)}
MESH = pl.DeviceIdType.MESH
F32 = jnp.float32
BF16 = jnp.bfloat16


def split(value):
    high = value.astype(BF16)
    return high, (value - high.astype(F32)).astype(BF16)


def mm(a, b):
    return jnp.dot(a, b, preferred_element_type=F32)


def mm3(a_high, a_low, b_high, b_low):
    return mm(a_high, b_high) + mm(a_low, b_high) + mm(a_high, b_low)


def kernel(
    dims,
    rhs_any,
    dinv_any,
    extract_any,
    lift_any,
    coef,
    nbr,
    colour,
    counts,
    send_lo,
    send_hi,
    rec_elem,
    rec_owner,
    rec_box,
    rec_weight,
    wall_map,
    fweights,
    grad,
    combined,
    rhs,
    dinv,
    extract,
    lift,
    ext_high,
    ext_low,
    lift_high,
    lift_low,
    psi,
    table,
    near_high,
    near_low,
    resid,
    sensed,
    out_up,
    out_down,
    in_below,
    in_above,
    tab_f,
    tab_i,
    sm_f,
    sm_i,
    tabs_in,
    boxes_i,
    sm_boxes,
    send_rec,
    recv_rec,
    z_send,
    z_recv,
    part,
    part_in,
    load_sem,
    dinv_sem,
    sm_sem,
    up_sem,
    down_sem,
    tab_sem,
    rec_sem,
    z_sem,
    fn_sem,
):
    X, Z, Y = dims
    XY = X * Y
    slots, funcs, width = rhs.shape
    rows = slots * funcs
    trace = extract.shape[1]
    rim = out_up.shape[1]
    records = rec_elem.shape[1]
    owners = X * Z * Y
    chunk = slots // dinv_sem.shape[0]
    me = lax.axis_index("dom")
    fn = lax.axis_index("fn")
    x = me // (Z * Y)
    z = (me // Y) % Z
    y = me % Y
    above = lax.rem(me + 1, owners)
    below = lax.rem(me + owners - 1, owners)

    def place(px, pz, py):
        return (px * Z + pz) * Y + py

    def plane_peer(rd):
        dx, dy = rd // Y, rd % Y
        return place(lax.rem(x + dx, X), z, lax.rem(y + dy, Y))

    def back(rd):
        dx, dy = rd // Y, rd % Y
        return ((X - dx) % X) * Y + (Y - dy) % Y

    half = Z // 2
    shifts = [half]
    for step in range(1, half):
        shifts += [half - step, half + step]
    shifts += [0]

    def column(j):
        return lax.rem(z + shifts[j], Z)

    small = []
    for i, (src, dst) in enumerate(
        ((rhs_any, rhs), (extract_any, extract), (lift_any, lift))
    ):
        copy = pltpu.make_async_copy(src, dst, load_sem.at[i])
        copy.start()
        small.append(copy)
    blocks = []
    for i in range(slots // chunk):
        span = pl.ds(i * chunk, chunk)
        copy = pltpu.make_async_copy(dinv_any.at[span], dinv.at[span], dinv_sem.at[i])
        copy.start()
        blocks.append(copy)

    barrier = pltpu.get_barrier_semaphore()
    partners = [(above, fn), (below, fn), (me, 1 - fn)]
    partners += [(plane_peer(rd), fn) for rd in range(1, XY)]
    partners += [(place(x, column(j), y), fn) for j in range(Z - 1)]
    for partner in partners:
        pl.semaphore_signal(barrier, inc=1, device_id=partner, device_id_type=MESH)

    lane = lax.broadcasted_iota(jnp.int32, (records, records), 1)
    sub = lax.broadcasted_iota(jnp.int32, (records, records), 0)
    own = jnp.broadcast_to(rec_owner[...], (records, records)).astype(F32)
    own_col = jnp.sum(jnp.where(lane == sub, own, 0.0), axis=1, keepdims=True)
    same = (own == own_col) & (lane < sub)
    rank = jnp.sum(jnp.where(same, 1.0, 0.0), axis=1, keepdims=True)
    lane_o = lax.broadcasted_iota(jnp.int32, (records, owners), 1).astype(F32)
    first = jnp.where((own_col == lane_o) & (rank < 0.5), 1.0, 0.0)
    second = jnp.where((own_col == lane_o) & (rank > 0.5), 1.0, 0.0)
    row = lax.broadcasted_iota(jnp.int32, (8, records), 0)
    elem_b = jnp.broadcast_to(rec_elem[...].astype(F32), (8, records))
    box_b = jnp.broadcast_to(rec_box[...].astype(F32), (8, records))
    weight_b = jnp.broadcast_to(rec_weight[...], (8, records))

    def rows_at(s):
        return jnp.where(
            row == s, box_b, jnp.where(row == 2 + s, elem_b, jnp.where(row == 4 + s, weight_b, 0.0))
        )

    tab = jnp.dot(
        rows_at(0), first, precision=lax.Precision.HIGHEST, preferred_element_type=F32
    ) + jnp.dot(
        rows_at(1), second, precision=lax.Precision.HIGHEST, preferred_element_type=F32
    )
    tab_f[...] = tab
    tab_i[...] = jnp.clip((tab + 0.25).astype(jnp.int32), 0, slots - 1)
    to_smem = [
        pltpu.make_async_copy(tab_f, sm_f, sm_sem.at[0]),
        pltpu.make_async_copy(tab_i, sm_i, sm_sem.at[1]),
    ]
    for copy in to_smem:
        copy.start()

    table[:, 0] = jnp.zeros((6, funcs, LANES), F32)
    small[1].wait()
    small[2].wait()
    for f in range(6):
        pad = jnp.zeros((LANES - trace, width), F32)
        value = jnp.concatenate([extract[OPPOSITE[f]], pad], axis=0)
        high, low = split(value.T)
        ext_high[:, f * LANES : (f + 1) * LANES] = high
        ext_low[:, f * LANES : (f + 1) * LANES] = low
        high, low = split(lift[f])
        pad = jnp.zeros((LANES - trace, width), BF16)
        lift_high[f * LANES : (f + 1) * LANES] = jnp.concatenate([high, pad], axis=0)
        lift_low[f * LANES : (f + 1) * LANES] = jnp.concatenate([low, pad], axis=0)

    pl.semaphore_wait(barrier, len(partners))
    tab_copies = []
    for rd in range(1, XY):
        copy = pltpu.make_async_remote_copy(
            src_ref=tab_f,
            dst_ref=tabs_in.at[back(rd)],
            send_sem=tab_sem.at[0, rd],
            recv_sem=tab_sem.at[1, back(rd)],
            device_id=(plane_peer(rd), fn),
            device_id_type=MESH,
        )
        copy.start()
        tab_copies.append(copy)

    live = counts[0]

    def update(e, shade, source, first_step):
        at = pl.ds(pl.multiple_of(e * funcs, funcs), funcs)
        value = source(e).astype(BF16)
        fresh = mm(value, dinv[e])
        mask = jnp.where((colour[e] == shade) & (e < live), 1, 0)
        old = jnp.zeros((funcs, width), F32) if first_step else psi[at]
        psi[at] = jnp.where(jnp.full((funcs, width), mask, jnp.int32) > 0, fresh, old)

    small[0].wait()
    for i, copy in enumerate(blocks):
        copy.wait()
        for k in range(chunk):
            update(i * chunk + k, 0, lambda e: rhs[e], True)

    exchanges = []
    for step in range(1, 2 * SWEEPS):
        shade = step % 2
        high, low = split(psi[...])

        def fill(pair):
            cols = pl.ds(pair * 2 * LANES, 2 * LANES)
            out = mm3(high, low, ext_high[:, cols], ext_low[:, cols])
            for half_ in range(2):
                table[pair * 2 + half_, 1 : slots + 1] = out[
                    :, half_ * LANES : (half_ + 1) * LANES
                ].reshape(slots, funcs, LANES)

        fill(0)
        for s in range(rim):
            out_up[step - 1, s] = table[0, send_hi[s] + 1]
            out_down[step - 1, s] = table[1, send_lo[s] + 1]
        up = pltpu.make_async_remote_copy(
            src_ref=out_up.at[step - 1],
            dst_ref=in_below.at[step - 1],
            send_sem=up_sem.at[0, step - 1],
            recv_sem=up_sem.at[1, step - 1],
            device_id=(above, fn),
            device_id_type=MESH,
        )
        up.start()
        down = pltpu.make_async_remote_copy(
            src_ref=out_down.at[step - 1],
            dst_ref=in_above.at[step - 1],
            send_sem=down_sem.at[0, step - 1],
            recv_sem=down_sem.at[1, step - 1],
            device_id=(below, fn),
            device_id_type=MESH,
        )
        down.start()
        exchanges += [up, down]
        fill(1)
        fill(2)

        def gather(faces):
            def pairs(i, _):
                for k in range(4):
                    e = i * 8 + k * 2
                    at = pl.ds(pl.multiple_of(e * funcs, 2 * funcs), 2 * funcs)
                    for f in faces:
                        value = jnp.concatenate(
                            [
                                table[f, nbr[f, e] + 1] * coef[f, e],
                                table[f, nbr[f, e + 1] + 1] * coef[f, e + 1],
                            ],
                            axis=0,
                        )
                        h, l = split(value)
                        near_high[at, f * LANES : (f + 1) * LANES] = h
                        near_low[at, f * LANES : (f + 1) * LANES] = l
                return 0

            lax.fori_loop(0, slots // 8, pairs, 0)

        def lifted(lo, hi):
            a, b = lo * LANES, hi * LANES
            return mm3(
                near_high[:, a:b], near_low[:, a:b], lift_high[a:b], lift_low[a:b]
            )

        gather((2, 3, 4, 5))
        resid[...] = rhs[...].reshape(rows, width) - lifted(2, 6)
        up.wait_recv()
        down.wait_recv()
        table[0, slots + 1 : slots + 1 + rim] = in_below[step - 1]
        table[1, slots + 1 + rim : slots + 1 + 2 * rim] = in_above[step - 1]
        gather((0, 1))
        resid[...] = resid[...] - lifted(0, 2)

        def source(e):
            return resid[pl.ds(pl.multiple_of(e * funcs, funcs), funcs)]

        def sweep(i, _):
            for k in range(8):
                update(i * 8 + k, shade, source, False)
            return 0

        lax.fori_loop(0, slots // 8, sweep, 0)

    high, low = split(psi[...])
    sensed[...] = (mm(high, wall_map[...]) + mm(low, wall_map[...])).reshape(
        slots, funcs, LANES
    )
    for copy in to_smem:
        copy.wait()
    for copy in tab_copies:
        copy.wait_recv()
    boxes_i[0] = tab_i[...]
    boxes_i[1:] = (tabs_in[1:] + 0.25).astype(jnp.int32)
    boxes = pltpu.make_async_copy(boxes_i, sm_boxes, sm_sem.at[2])
    boxes.start()
    per = rec_sem.shape[1]
    group = Z // per
    rec_copies = []
    for c in range(per):

        def build(rd, _):
            px, py = lax.rem(x + rd // Y, X), lax.rem(y + rd % Y, Y)
            for j in range(c * group, (c + 1) * group):
                owner = place(px, column(j), py)
                for s in range(2):
                    send_rec[rd, j, s] = sensed[sm_i[2 + s, owner]] * sm_f[4 + s, owner]
            return 0

        lax.fori_loop(0, XY, build, 0)
        span = pl.ds(c * group, group)
        sent = []
        for rd in range(1, XY):
            copy = pltpu.make_async_remote_copy(
                src_ref=send_rec.at[rd, span],
                dst_ref=recv_rec.at[back(rd), span],
                send_sem=rec_sem.at[0, c, rd],
                recv_sem=rec_sem.at[1, c, back(rd)],
                device_id=(plane_peer(rd), fn),
                device_id_type=MESH,
            )
            copy.start()
            sent.append(copy)
        rec_copies.append(sent)
    boxes.wait()

    z_copies = []
    for c in range(per):
        for copy in rec_copies[c]:
            copy.wait_recv()
        for j in range(c * group, (c + 1) * group):
            owner = place(x, column(j), y)

            def add(value, box, total):
                which = jnp.full((funcs, LANES), box, jnp.int32)
                return tuple(t + jnp.where(which == b, value, 0.0) for b, t in enumerate(total))

            total = (jnp.zeros((funcs, LANES), F32),) * BOX_DEV
            for s in range(2):
                total = add(send_rec[0, j, s], sm_boxes[0, s, owner], total)

            def accumulate(rd, total):
                for s in range(2):
                    total = add(recv_rec[rd, j, s], sm_boxes[rd, s, owner], total)
                return total

            total = lax.fori_loop(1, XY, accumulate, total)
            for b in range(BOX_DEV):
                z_send[j, b] = total[b]
            if j < Z - 1:
                far = shifts.index((Z - shifts[j]) % Z)
                copy = pltpu.make_async_remote_copy(
                    src_ref=z_send.at[j],
                    dst_ref=z_recv.at[far],
                    send_sem=z_sem.at[0, j],
                    recv_sem=z_sem.at[1, far],
                    device_id=(place(x, column(j), y), fn),
                    device_id_type=MESH,
                )
                copy.start()
                z_copies.append(copy)

    result = z_send[Z - 1]
    for copy in z_copies:
        copy.wait_recv()
    for j in range(Z - 1):
        result = result + z_recv[j]
    grad[...] = result

    sub_f = lax.broadcasted_iota(jnp.int32, (funcs, LANES), 0)
    scale = jnp.zeros((funcs, LANES), F32)
    for j in range(funcs):
        scale = jnp.where(sub_f == j, fweights[j], scale)
    part[...] = jnp.sum(result * scale[None], axis=1)
    pair = pltpu.make_async_remote_copy(
        src_ref=part,
        dst_ref=part_in,
        send_sem=fn_sem.at[0],
        recv_sem=fn_sem.at[1],
        device_id=(me, 1 - fn),
        device_id_type=MESH,
    )
    pair.start()
    pair.wait_recv()
    combined[...] = part[...] + part_in[...]

    pair.wait_send()
    for copy in tab_copies + exchanges + z_copies:
        copy.wait_send()
    for sent in rec_copies:
        for copy in sent:
            copy.wait_send()


def body(
    rhs,
    dinv,
    extract,
    lift,
    coef,
    nbr,
    colour,
    counts,
    send_lo,
    send_hi,
    rec_elem,
    rec_owner,
    rec_box,
    rec_weight,
    wall_map,
    fweights,
):
    slots, funcs, width = rhs.shape
    rim = send_lo.shape[0]
    records = rec_elem.shape[0]
    owners = lax.axis_size("dom")
    X, Z, Y = GRIDS[owners]
    rows = slots * funcs
    steps = 2 * SWEEPS - 1
    blocks = 8
    per = min(4, Z)
    any_ = pl.BlockSpec(memory_space=pl.ANY)
    smem = pl.BlockSpec(memory_space=pltpu.SMEM)
    vmem = pl.BlockSpec(memory_space=pltpu.VMEM)
    dma = pltpu.SemaphoreType.DMA
    return pl.pallas_call(
        functools.partial(kernel, (X, Z, Y)),
        out_shape=(
            jax.ShapeDtypeStruct((BOX_DEV, funcs, LANES), F32),
            jax.ShapeDtypeStruct((BOX_DEV, LANES), F32),
        ),
        in_specs=[any_] * 4 + [smem] * 6 + [vmem] * 5 + [smem],
        out_specs=(vmem, vmem),
        scratch_shapes=[
            pltpu.VMEM(rhs.shape, F32),
            pltpu.VMEM(dinv.shape, BF16),
            pltpu.VMEM(lift.shape, F32),
            pltpu.VMEM(lift.shape, F32),
            pltpu.VMEM((width, 6 * LANES), BF16),
            pltpu.VMEM((width, 6 * LANES), BF16),
            pltpu.VMEM((6 * LANES, width), BF16),
            pltpu.VMEM((6 * LANES, width), BF16),
            pltpu.VMEM((rows, width), F32),
            pltpu.VMEM((6, slots + 2 * rim + 1, funcs, LANES), F32),
            pltpu.VMEM((rows, 6 * LANES), BF16),
            pltpu.VMEM((rows, 6 * LANES), BF16),
            pltpu.VMEM((rows, width), F32),
            pltpu.VMEM((slots, funcs, LANES), F32),
            pltpu.VMEM((steps, rim, funcs, LANES), F32),
            pltpu.VMEM((steps, rim, funcs, LANES), F32),
            pltpu.VMEM((steps, rim, funcs, LANES), F32),
            pltpu.VMEM((steps, rim, funcs, LANES), F32),
            pltpu.VMEM((8, owners), F32),
            pltpu.VMEM((8, owners), jnp.int32),
            pltpu.SMEM((8, owners), F32),
            pltpu.SMEM((8, owners), jnp.int32),
            pltpu.VMEM((X * Y, 8, owners), F32),
            pltpu.VMEM((X * Y, 8, owners), jnp.int32),
            pltpu.SMEM((X * Y, 8, owners), jnp.int32),
            pltpu.VMEM((X * Y, Z, 2, funcs, LANES), F32),
            pltpu.VMEM((X * Y, Z, 2, funcs, LANES), F32),
            pltpu.VMEM((Z, BOX_DEV, funcs, LANES), F32),
            pltpu.VMEM((Z, BOX_DEV, funcs, LANES), F32),
            pltpu.VMEM((BOX_DEV, LANES), F32),
            pltpu.VMEM((BOX_DEV, LANES), F32),
            dma((3,)),
            dma((blocks,)),
            dma((3,)),
            dma((2, steps)),
            dma((2, steps)),
            dma((2, X * Y)),
            dma((2, per, X * Y)),
            dma((2, Z)),
            dma((2,)),
        ],
        compiler_params=pltpu.CompilerParams(
            collective_id=0, has_side_effects=True, vmem_limit_bytes=48 * 1024 * 1024
        ),
    )(
        rhs,
        dinv,
        extract.transpose(0, 2, 1),
        lift,
        coef.T,
        nbr.T,
        colour,
        counts,
        send_lo,
        send_hi,
        rec_elem.reshape(1, records),
        rec_owner.T,
        rec_box.reshape(1, records),
        rec_weight.reshape(1, records),
        wall_map,
        fweights,
    )


def solution(mesh):
    placed = (
        P("dom", "fn", None),
        P("dom", None, None),
        P(),
        P(),
        P("dom", None),
        P("dom", None),
        P("dom"),
        P("dom"),
        P("dom"),
        P("dom"),
        P("dom"),
        P("dom", None),
        P("dom"),
        P("dom"),
        P(),
        P("fn"),
    )
    return jax.shard_map(
        body,
        mesh=mesh,
        in_specs=placed,
        out_specs=(P("dom", "fn", None), P("dom", None)),
        check_vma=False,
    )
```

```python
import functools
import jax
import jax.numpy as jnp
from jax import lax
from jax.experimental import pallas as pl
from jax.experimental.pallas import tpu as pltpu
from jax.sharding import PartitionSpec as P

BOX_DEV = 4
SWEEPS = 2
OPPOSITE = (1, 0, 3, 2, 5, 4)
LANES = 128
GRIDS = {128: (4, 8, 4), 8: (2, 2, 2)}
MESH = pl.DeviceIdType.MESH
F32 = jnp.float32
BF16 = jnp.bfloat16


def split(value):
    high = value.astype(BF16)
    return high, (value - high.astype(F32)).astype(BF16)


def mm(a, b):
    return jnp.dot(a, b, preferred_element_type=F32)


def kernel(
    dims,
    rhs_hbm,
    dinv_hbm,
    extract_hbm,
    lift_hbm,
    coef_hbm,
    nbr_hbm,
    colour_hbm,
    counts_hbm,
    send_lo_hbm,
    send_hi_hbm,
    rec_elem_hbm,
    rec_owner_hbm,
    rec_box_hbm,
    rec_weight_hbm,
    wall_map_hbm,
    fweights_hbm,
    grad,
    combined,
    rhs,
    dinv,
    extract,
    lift,
    coef,
    nbr,
    colour,
    counts,
    send_lo,
    send_hi,
    rec_elem,
    rec_owner,
    rec_box,
    rec_weight,
    wall_map,
    fweights,
    ext_cat,
    lift_cat,
    psi,
    table,
    scale,
    near_high,
    near_low,
    resid,
    sensed,
    out_up,
    out_down,
    in_below,
    in_above,
    tab_f,
    tab_i,
    sm_f,
    sm_i,
    tabs_in,
    boxes_i,
    sm_boxes,
    send_rec,
    recv_rec,
    z_send,
    z_recv,
    part,
    part_in,
    load_sem,
    dinv_sem,
    sm_sem,
    up_sem,
    down_sem,
    tab_sem,
    rec_sem,
    z_sem,
    fn_sem,
):
    X, Z, Y = dims
    XY = X * Y
    slots, funcs, width = rhs.shape
    rows = slots * funcs
    trace = extract.shape[1]
    rim = out_up.shape[1]
    records = rec_elem.shape[1]
    owners = X * Z * Y
    chunk = slots // dinv_sem.shape[0]
    me = lax.axis_index("dom")
    fn = lax.axis_index("fn")
    x = me // (Z * Y)
    z = (me // Y) % Z
    y = me % Y
    above = lax.rem(me + 1, owners)
    below = lax.rem(me + owners - 1, owners)

    def place(px, pz, py):
        return (px * Z + pz) * Y + py

    def plane_peer(rd):
        dx, dy = rd // Y, rd % Y
        return place(lax.rem(x + dx, X), z, lax.rem(y + dy, Y))

    def wait_for(ref, sem):
        pltpu.make_async_copy(ref, ref, sem).wait()

    def back(rd):
        dx, dy = rd // Y, rd % Y
        return ((X - dx) % X) * Y + (Y - dy) % Y

    half = Z // 2
    shifts = [half]
    for step in range(1, half):
        shifts += [half - step, half + step]
    shifts += [0]

    def column(j):
        return lax.rem(z + shifts[j], Z)

    order = (
        (rec_owner_hbm, rec_owner),
        (rec_elem_hbm, rec_elem),
        (rec_box_hbm, rec_box),
        (rec_weight_hbm, rec_weight),
        (colour_hbm, colour),
        (counts_hbm, counts),
        (coef_hbm, coef),
        (nbr_hbm, nbr),
        (send_lo_hbm, send_lo),
        (send_hi_hbm, send_hi),
        (rhs_hbm, rhs),
        (extract_hbm, extract),
        (lift_hbm, lift),
        (wall_map_hbm, wall_map),
        (fweights_hbm, fweights),
    )
    small = []
    for i, (src, dst) in enumerate(order):
        copy = pltpu.make_async_copy(src, dst, load_sem.at[i])
        copy.start()
        small.append(copy)
    blocks = []
    for i in range(slots // chunk):
        span = pl.ds(i * chunk, chunk)
        copy = pltpu.make_async_copy(dinv_hbm.at[span], dinv.at[span], dinv_sem.at[i])
        copy.start()
        blocks.append(copy)

    barrier = pltpu.get_barrier_semaphore()
    partners = [(above, fn), (below, fn), (me, 1 - fn)]
    partners += [(plane_peer(rd), fn) for rd in range(1, XY)]
    partners += [(place(x, column(j), y), fn) for j in range(Z - 1)]
    partners += [(place(x, column(j), y), 1 - fn) for j in range(Z - 1)]
    for partner in partners:
        pl.semaphore_signal(barrier, inc=1, device_id=partner, device_id_type=MESH)

    for copy in small[:4]:
        copy.wait()
    lane = lax.broadcasted_iota(jnp.int32, (records, records), 1)
    sub = lax.broadcasted_iota(jnp.int32, (records, records), 0)
    own = jnp.broadcast_to(rec_owner[...], (records, records)).astype(F32)
    own_col = jnp.sum(jnp.where(lane == sub, own, 0.0), axis=1, keepdims=True)
    same = (own == own_col) & (lane < sub)
    rank = jnp.sum(jnp.where(same, 1.0, 0.0), axis=1, keepdims=True)
    lane_o = lax.broadcasted_iota(jnp.int32, (records, owners), 1).astype(F32)
    first = jnp.where((own_col == lane_o) & (rank < 0.5), 1.0, 0.0)
    second = jnp.where((own_col == lane_o) & (rank > 0.5), 1.0, 0.0)
    row = lax.broadcasted_iota(jnp.int32, (8, records), 0)
    elem_b = jnp.broadcast_to(rec_elem[...].astype(F32), (8, records))
    box_b = jnp.broadcast_to(rec_box[...].astype(F32), (8, records))
    weight_b = jnp.broadcast_to(rec_weight[...], (8, records))

    def rows_at(s):
        return jnp.where(
            row == s, box_b, jnp.where(row == 2 + s, elem_b, jnp.where(row == 4 + s, weight_b, 0.0))
        )

    tab = jnp.dot(
        rows_at(0), first, precision=lax.Precision.HIGHEST, preferred_element_type=F32
    ) + jnp.dot(
        rows_at(1), second, precision=lax.Precision.HIGHEST, preferred_element_type=F32
    )
    tab_f[...] = tab
    tab_i[...] = jnp.clip((tab + 0.25).astype(jnp.int32), 0, slots - 1)
    to_smem = [
        pltpu.make_async_copy(tab_f, sm_f, sm_sem.at[0]),
        pltpu.make_async_copy(tab_i, sm_i, sm_sem.at[1]),
    ]
    for copy in to_smem:
        copy.start()

    full = width // (2 * LANES) * 2 * LANES
    table[:, 0] = jnp.zeros((6, funcs, LANES), F32)
    small[11].wait()
    small[12].wait()
    for f in range(6):
        pad = jnp.zeros((LANES - trace, width), F32)
        value = jnp.concatenate([extract[OPPOSITE[f]], pad], axis=0)
        high, low = split(value.T)
        cols = slice(f * LANES, (f + 1) * LANES)
        pieces = [high[:full], high[:full], low[:full], high[full:], high[full:], low[full:]]
        if 3 * width < ext_cat.shape[0]:
            pieces += [jnp.zeros((ext_cat.shape[0] - 3 * width, LANES), BF16)]
        ext_cat[:, cols] = jnp.concatenate(pieces, axis=0)
        pad = jnp.zeros((LANES - trace, width), F32)
        high, low = split(jnp.concatenate([lift[f], pad], axis=0))
        lift_cat[0, f * LANES : (f + 1) * LANES] = high
        lift_cat[1, f * LANES : (f + 1) * LANES] = low

    small[6].wait()

    def spread(i, _):
        for k in range(8):
            for f in range(6):
                scale[f, i * 8 + k] = jnp.full((funcs, LANES), coef[f, i * 8 + k], F32)
        return 0

    lax.fori_loop(0, slots // 8, spread, 0)
    small[4].wait()
    small[5].wait()
    live = counts[0]
    batch = slots // 2

    def update(first_e, count, shade, source, first_step):
        fresh = []
        for k in range(count):
            value = source(first_e + k).astype(BF16)
            fresh.append(mm(value, dinv[first_e + k]))
        for k in range(count):
            e = first_e + k
            mask = jnp.where((colour[e] == shade) & (e < live), 1, 0)
            mask = jnp.full((funcs, width), mask, jnp.int32) > 0
            at = pl.ds(pl.multiple_of(e * funcs, funcs), funcs)
            old = jnp.zeros((funcs, width), F32) if first_step else psi[at]
            psi[at] = jnp.where(mask, fresh[k], old)

    small[10].wait()

    def start(i, _):
        span = pl.ds(i * chunk, chunk)
        pltpu.make_async_copy(dinv_hbm.at[span], dinv.at[span], dinv_sem.at[i]).wait()
        update(i * chunk, chunk, 0, lambda e: rhs[e], True)
        return 0

    lax.fori_loop(0, slots // chunk, start, 0)

    for i in (7, 8, 9, 13, 14):
        small[i].wait()
    pl.semaphore_wait(barrier, len(partners))
    def step_body(step, _):
        shade = lax.rem(step, 2)
        high, low = split(psi[...])
        pieces = [high[:, :full], low[:, :full], high[:, :full]]
        pieces += [high[:, full:], low[:, full:], high[:, full:]]
        if 3 * width < ext_cat.shape[0]:
            pieces += [jnp.zeros((rows, ext_cat.shape[0] - 3 * width), BF16)]
        state = jnp.concatenate(pieces, axis=1)

        def fill(pair):
            cols = pl.ds(pair * 2 * LANES, 2 * LANES)
            out = mm(state, ext_cat[:, cols])
            for half_ in range(2):
                table[pair * 2 + half_, 1 : slots + 1] = out[
                    :, half_ * LANES : (half_ + 1) * LANES
                ].reshape(slots, funcs, LANES)

        fill(0)
        for s in range(rim):
            out_up[step - 1, s] = table[0, send_hi[s] + 1]
            out_down[step - 1, s] = table[1, send_lo[s] + 1]
        up = pltpu.make_async_remote_copy(
            src_ref=out_up.at[step - 1],
            dst_ref=in_below.at[step - 1],
            send_sem=up_sem.at[0],
            recv_sem=up_sem.at[step],
            device_id=(above, fn),
            device_id_type=MESH,
        )
        up.start()
        down = pltpu.make_async_remote_copy(
            src_ref=out_down.at[step - 1],
            dst_ref=in_above.at[step - 1],
            send_sem=down_sem.at[0],
            recv_sem=down_sem.at[step],
            device_id=(below, fn),
            device_id_type=MESH,
        )
        down.start()
        fill(1)
        fill(2)

        def gather(faces):
            def pairs(i, _):
                for f in faces:
                    found = []
                    for k in range(4):
                        e = i * 8 + k * 2
                        found.append(
                            jnp.concatenate(
                                [
                                    table[f, nbr[f, e] + 1] * scale[f, e],
                                    table[f, nbr[f, e + 1] + 1] * scale[f, e + 1],
                                ],
                                axis=0,
                            )
                        )
                    found = [split(value) for value in found]
                    for k in range(4):
                        start = pl.multiple_of((i * 8 + k * 2) * funcs, 2 * funcs)
                        at = pl.ds(start, 2 * funcs)
                        near_high[at, f * LANES : (f + 1) * LANES] = found[k][0]
                        near_low[at, f * LANES : (f + 1) * LANES] = found[k][1]
                return 0

            lax.fori_loop(0, slots // 8, pairs, 0)

        def lifted(lo, hi):
            a, b = lo * LANES, hi * LANES
            left = jnp.concatenate([near_high[:, a:b], near_low[:, a:b], near_high[:, a:b]], axis=1)
            right = jnp.concatenate([lift_cat[0, a:b], lift_cat[0, a:b], lift_cat[1, a:b]], axis=0)
            return mm(left, right)

        gather((2, 3, 4, 5))
        resid[...] = rhs[...].reshape(rows, width) - lifted(2, 6)
        up.wait_recv()
        down.wait_recv()
        table[0, slots + 1 : slots + 1 + rim] = in_below[step - 1]
        table[1, slots + 1 + rim : slots + 1 + 2 * rim] = in_above[step - 1]
        gather((0, 1))
        resid[...] = resid[...] - lifted(0, 2)

        def source(e):
            return resid[pl.ds(pl.multiple_of(e * funcs, funcs), funcs)]

        def sweep(i, _):
            update(i * batch, batch, shade, source, False)
            return 0

        lax.fori_loop(0, slots // batch, sweep, 0)
        up.wait_send()
        down.wait_send()
        return 0

    lax.fori_loop(1, 2 * SWEEPS, step_body, 0)

    for rd in range(1, XY):
        copy = pltpu.make_async_remote_copy(
            src_ref=tab_f,
            dst_ref=tabs_in.at[back(rd)],
            send_sem=tab_sem.at[0],
            recv_sem=tab_sem.at[1],
            device_id=(plane_peer(rd), fn),
            device_id_type=MESH,
        )
        copy.start()
    high, low = split(psi[...])
    sensed[...] = (mm(high, wall_map[...]) + mm(low, wall_map[...])).reshape(
        slots, funcs, LANES
    )
    for copy in to_smem:
        copy.wait()
    wait_for(tabs_in.at[1:], tab_sem.at[1])
    boxes_i[0] = tab_i[...]
    boxes_i[1:] = (tabs_in[1:] + 0.25).astype(jnp.int32)
    boxes = pltpu.make_async_copy(boxes_i, sm_boxes, sm_sem.at[2])
    boxes.start()
    per = rec_sem.shape[0] - 1
    group = Z // per
    for c in range(per):

        def build(rd, _):
            px, py = lax.rem(x + rd // Y, X), lax.rem(y + rd % Y, Y)
            for j in range(c * group, (c + 1) * group):
                owner = place(px, column(j), py)
                for s in range(2):
                    send_rec[rd, j, s] = sensed[sm_i[2 + s, owner]] * sm_f[4 + s, owner]
            return 0

        lax.fori_loop(0, XY, build, 0)
        span = pl.ds(c * group, group)
        for rd in range(1, XY):
            copy = pltpu.make_async_remote_copy(
                src_ref=send_rec.at[rd, span],
                dst_ref=recv_rec.at[back(rd), span],
                send_sem=rec_sem.at[per],
                recv_sem=rec_sem.at[c],
                device_id=(plane_peer(rd), fn),
                device_id_type=MESH,
            )
            copy.start()
    boxes.wait()

    sub_f = lax.broadcasted_iota(jnp.int32, (funcs, LANES), 0)
    weight = jnp.zeros((funcs, LANES), F32)
    for j in range(funcs):
        weight = jnp.where(sub_f == j, fweights[j], weight)
    for c in range(per):
        wait_for(recv_rec.at[1:, pl.ds(c * group, group)], rec_sem.at[c])
        for j in range(c * group, (c + 1) * group):
            owner = place(x, column(j), y)

            def add(value, box, total):
                which = jnp.full((funcs, LANES), box, jnp.int32)
                return tuple(t + jnp.where(which == b, value, 0.0) for b, t in enumerate(total))

            total = (jnp.zeros((funcs, LANES), F32),) * BOX_DEV
            for s in range(2):
                total = add(send_rec[0, j, s], sm_boxes[0, s, owner], total)

            def accumulate(rd, total):
                for s in range(2):
                    total = add(recv_rec[rd, j, s], sm_boxes[rd, s, owner], total)
                return total

            total = lax.fori_loop(1, XY, accumulate, total)
            for b in range(BOX_DEV):
                z_send[j, b] = total[b]
            far = shifts.index((Z - shifts[j]) % Z)
            part[j] = jnp.concatenate(
                [jnp.sum(total[b] * weight, axis=0, keepdims=True) for b in range(BOX_DEV)], axis=0
            )
            copy = pltpu.make_async_remote_copy(
                src_ref=part.at[j],
                dst_ref=part_in.at[far],
                send_sem=fn_sem.at[0],
                recv_sem=fn_sem.at[1],
                device_id=(place(x, column(j), y), 1 - fn),
                device_id_type=MESH,
            )
            copy.start()
            if j < Z - 1:
                copy = pltpu.make_async_remote_copy(
                    src_ref=z_send.at[j],
                    dst_ref=z_recv.at[far],
                    send_sem=z_sem.at[0],
                    recv_sem=z_sem.at[1],
                    device_id=(place(x, column(j), y), fn),
                    device_id_type=MESH,
                )
                copy.start()

    result = z_send[Z - 1]
    wait_for(z_recv.at[: Z - 1], z_sem.at[1])
    wait_for(part_in, fn_sem.at[1])
    for j in range(Z - 1):
        result = result + z_recv[j]
    grad[...] = result

    own_part = jnp.sum(result * weight[None], axis=1)
    for j in range(Z):
        own_part = own_part + part_in[j]
    combined[...] = own_part

    wait_for(tabs_in.at[1:], tab_sem.at[0])
    wait_for(send_rec.at[1:], rec_sem.at[per])
    wait_for(z_send.at[: Z - 1], z_sem.at[0])
    wait_for(part, fn_sem.at[0])


def body(
    rhs,
    dinv,
    extract,
    lift,
    coef,
    nbr,
    colour,
    counts,
    send_lo,
    send_hi,
    rec_elem,
    rec_owner,
    rec_box,
    rec_weight,
    wall_map,
    fweights,
):
    slots, funcs, width = rhs.shape
    rim = send_lo.shape[0]
    records = rec_elem.shape[0]
    owners = lax.axis_size("dom")
    X, Z, Y = GRIDS[owners]
    rows = slots * funcs
    steps = 2 * SWEEPS - 1
    blocks = 8
    per = min(4, Z)
    hbm = pl.BlockSpec(memory_space=pltpu.HBM)
    vmem = pl.BlockSpec(memory_space=pltpu.VMEM)
    dma = pltpu.SemaphoreType.DMA
    return pl.pallas_call(
        functools.partial(kernel, (X, Z, Y)),
        out_shape=(
            jax.ShapeDtypeStruct((BOX_DEV, funcs, LANES), F32),
            jax.ShapeDtypeStruct((BOX_DEV, LANES), F32),
        ),
        in_specs=[hbm] * 16,
        out_specs=(vmem, vmem),
        scratch_shapes=[
            pltpu.VMEM(rhs.shape, F32),
            pltpu.VMEM(dinv.shape, BF16),
            pltpu.VMEM(lift.shape, F32),
            pltpu.VMEM(lift.shape, F32),
            pltpu.SMEM((6, slots), F32),
            pltpu.SMEM((6, slots), jnp.int32),
            pltpu.SMEM((slots,), jnp.int32),
            pltpu.SMEM((1,), jnp.int32),
            pltpu.SMEM((rim,), jnp.int32),
            pltpu.SMEM((rim,), jnp.int32),
            pltpu.VMEM((1, records), jnp.int32),
            pltpu.VMEM((1, records), jnp.int32),
            pltpu.VMEM((1, records), jnp.int32),
            pltpu.VMEM((1, records), F32),
            pltpu.VMEM(wall_map.shape, BF16),
            pltpu.SMEM((funcs,), F32),
            pltpu.VMEM((pl.cdiv(3 * width, 2 * LANES) * 2 * LANES, 6 * LANES), BF16),
            pltpu.VMEM((2, 6 * LANES, width), BF16),
            pltpu.VMEM((rows, width), F32),
            pltpu.VMEM((6, slots + 2 * rim + 1, funcs, LANES), F32),
            pltpu.VMEM((6, slots, funcs, LANES), F32),
            pltpu.VMEM((rows, 6 * LANES), BF16),
            pltpu.VMEM((rows, 6 * LANES), BF16),
            pltpu.VMEM((rows, width), F32),
            pltpu.VMEM((slots, funcs, LANES), F32),
            pltpu.VMEM((steps, rim, funcs, LANES), F32),
            pltpu.VMEM((steps, rim, funcs, LANES), F32),
            pltpu.VMEM((steps, rim, funcs, LANES), F32),
            pltpu.VMEM((steps, rim, funcs, LANES), F32),
            pltpu.VMEM((8, owners), F32),
            pltpu.VMEM((8, owners), jnp.int32),
            pltpu.SMEM((8, owners), F32),
            pltpu.SMEM((8, owners), jnp.int32),
            pltpu.VMEM((X * Y, 8, owners), F32),
            pltpu.VMEM((X * Y, 8, owners), jnp.int32),
            pltpu.SMEM((X * Y, 8, owners), jnp.int32),
            pltpu.VMEM((X * Y, Z, 2, funcs, LANES), F32),
            pltpu.VMEM((X * Y, Z, 2, funcs, LANES), F32),
            pltpu.VMEM((Z, BOX_DEV, funcs, LANES), F32),
            pltpu.VMEM((Z, BOX_DEV, funcs, LANES), F32),
            pltpu.VMEM((Z, BOX_DEV, LANES), F32),
            pltpu.VMEM((Z, BOX_DEV, LANES), F32),
            dma((15,)),
            dma((blocks,)),
            dma((3,)),
            dma((1 + steps,)),
            dma((1 + steps,)),
            dma((2,)),
            dma((per + 1,)),
            dma((2,)),
            dma((2,)),
        ],
        compiler_params=pltpu.CompilerParams(
            collective_id=0, has_side_effects=True, vmem_limit_bytes=64 * 1024 * 1024
        ),
    )(
        rhs,
        dinv,
        extract.transpose(0, 2, 1),
        lift,
        coef.T,
        nbr.T,
        colour,
        counts,
        send_lo,
        send_hi,
        rec_elem.reshape(1, records),
        rec_owner.T,
        rec_box.reshape(1, records),
        rec_weight.reshape(1, records),
        wall_map,
        fweights,
    )


def solution(mesh):
    placed = (
        P("dom", "fn", None),
        P("dom", None, None),
        P(),
        P(),
        P("dom", None),
        P("dom", None),
        P("dom"),
        P("dom"),
        P("dom"),
        P("dom"),
        P("dom"),
        P("dom", None),
        P("dom"),
        P("dom"),
        P(),
        P("fn"),
    )
    return jax.shard_map(
        body,
        mesh=mesh,
        in_specs=placed,
        out_specs=(P("dom", "fn", None), P("dom", None)),
        check_vma=False,
    )
```

```python
import functools
import jax
import jax.numpy as jnp
from jax import lax
from jax.experimental import pallas as pl
from jax.experimental.pallas import tpu as pltpu
from jax.sharding import PartitionSpec as P

BOX_DEV = 4
SWEEPS = 2
OPPOSITE = (1, 0, 3, 2, 5, 4)
LANES = 128
GRIDS = {128: (4, 8, 4), 8: (2, 2, 2)}
MESH = pl.DeviceIdType.MESH
F32 = jnp.float32
BF16 = jnp.bfloat16


def split(value):
    high = value.astype(BF16)
    return high, (value - high.astype(F32)).astype(BF16)


def mm(a, b):
    return jnp.dot(a, b, preferred_element_type=F32)


def far_displacements(X, Y):
    def hops(rd):
        dx, dy = rd // Y, rd % Y
        return min(dx, X - dx) + min(dy, Y - dy)

    longest = 3 if X == 4 else 2
    return [rd for rd in range(X * Y) if hops(rd) == longest]


def hand_over(grad_in, combined_in, grad, combined, sem):
    copies = [
        pltpu.make_async_copy(grad_in, grad, sem.at[0]),
        pltpu.make_async_copy(combined_in, combined, sem.at[1]),
    ]
    for copy in copies:
        copy.start()
    for copy in copies:
        copy.wait()


def kernel(
    dims,
    rhs_hbm,
    dinv_hbm,
    extract_hbm,
    lift_hbm,
    coef_hbm,
    nbr_hbm,
    colour_hbm,
    counts_hbm,
    send_lo_hbm,
    send_hi_hbm,
    rec_elem_hbm,
    rec_owner_hbm,
    rec_box_hbm,
    rec_weight_hbm,
    wall_map_hbm,
    fweights_hbm,
    grad,
    combined,
    rhs,
    dinv,
    extract,
    lift,
    coef,
    nbr,
    colour,
    counts,
    send_lo,
    send_hi,
    rec_elem,
    rec_owner,
    rec_box,
    rec_weight,
    wall_map,
    fweights,
    ext_cat,
    lift_cat,
    psi,
    table,
    scale,
    near_high,
    near_low,
    resid,
    sensed,
    out_up,
    out_down,
    in_below,
    in_above,
    tab_f,
    tab_i,
    sm_f,
    sm_i,
    tabs_in,
    boxes_i,
    sm_boxes,
    send_rec,
    recv_rec,
    z_send,
    z_recv,
    part,
    part_in,
    far_send,
    far_recv,
    last_send,
    last_recv,
    last_part,
    last_part_in,
    load_sem,
    dinv_sem,
    sm_sem,
    up_sem,
    down_sem,
    tab_sem,
    rec_sem,
    z_sem,
    far_sem,
    last_sem,
):
    X, Z, Y = dims
    XY = X * Y
    slots, funcs, width = rhs.shape
    rows = slots * funcs
    trace = extract.shape[1]
    rim = out_up.shape[1]
    records = rec_elem.shape[1]
    owners = X * Z * Y
    chunk = slots // dinv_sem.shape[0]
    me = lax.axis_index("dom")
    fn = lax.axis_index("fn")
    x = me // (Z * Y)
    z = (me // Y) % Z
    y = me % Y
    above = lax.rem(me + 1, owners)
    below = lax.rem(me + owners - 1, owners)

    def place(px, pz, py):
        return (px * Z + pz) * Y + py

    def plane_peer(rd):
        dx, dy = rd // Y, rd % Y
        return place(lax.rem(x + dx, X), z, lax.rem(y + dy, Y))

    def wait_for(ref, sem):
        pltpu.make_async_copy(ref, ref, sem).wait()

    def back(rd):
        dx, dy = rd // Y, rd % Y
        return ((X - dx) % X) * Y + (Y - dy) % Y

    far_first = far_displacements(X, Y)
    near_first = [rd for rd in range(XY) if rd not in far_first]
    A, B = len(near_first), len(far_first)

    half = Z // 2
    shifts = [half]
    for step in range(1, half):
        shifts += [half - step, half + step]
    shifts += [0]

    def column(j):
        return lax.rem(z + shifts[j], Z)

    def opposite(j):
        return shifts.index((Z - shifts[j]) % Z)

    order = (
        (rec_owner_hbm, rec_owner),
        (rec_elem_hbm, rec_elem),
        (rec_box_hbm, rec_box),
        (rec_weight_hbm, rec_weight),
        (colour_hbm, colour),
        (counts_hbm, counts),
        (coef_hbm, coef),
        (nbr_hbm, nbr),
        (send_lo_hbm, send_lo),
        (send_hi_hbm, send_hi),
        (rhs_hbm, rhs),
        (extract_hbm, extract),
        (lift_hbm, lift),
        (wall_map_hbm, wall_map),
        (fweights_hbm, fweights),
    )
    small = []
    for i, (src, dst) in enumerate(order):
        copy = pltpu.make_async_copy(src, dst, load_sem.at[i])
        copy.start()
        small.append(copy)
    blocks = []
    for i in range(slots // chunk):
        span = pl.ds(i * chunk, chunk)
        copy = pltpu.make_async_copy(dinv_hbm.at[span], dinv.at[span], dinv_sem.at[i])
        copy.start()
        blocks.append(copy)

    barrier = pltpu.get_barrier_semaphore()
    partners = [(above, fn), (below, fn), (me, 1 - fn)]
    partners += [(plane_peer(rd), fn) for rd in range(1, XY)]
    partners += [(plane_peer(rd), 1 - fn) for rd in far_first]
    partners += [(place(x, column(j), y), fn) for j in range(Z - 1)]
    partners += [(place(x, column(j), y), 1 - fn) for j in range(Z - 1)]
    for partner in partners:
        pl.semaphore_signal(barrier, inc=1, device_id=partner, device_id_type=MESH)

    for copy in small[:4]:
        copy.wait()
    lane = lax.broadcasted_iota(jnp.int32, (records, records), 1)
    sub = lax.broadcasted_iota(jnp.int32, (records, records), 0)
    own = jnp.broadcast_to(rec_owner[...], (records, records)).astype(F32)
    own_col = jnp.sum(jnp.where(lane == sub, own, 0.0), axis=1, keepdims=True)
    same = (own == own_col) & (lane < sub)
    rank = jnp.sum(jnp.where(same, 1.0, 0.0), axis=1, keepdims=True)
    lane_o = lax.broadcasted_iota(jnp.int32, (records, owners), 1).astype(F32)
    first = jnp.where((own_col == lane_o) & (rank < 0.5), 1.0, 0.0)
    second = jnp.where((own_col == lane_o) & (rank > 0.5), 1.0, 0.0)
    row = lax.broadcasted_iota(jnp.int32, (8, records), 0)
    elem_b = jnp.broadcast_to(rec_elem[...].astype(F32), (8, records))
    box_b = jnp.broadcast_to(rec_box[...].astype(F32), (8, records))
    weight_b = jnp.broadcast_to(rec_weight[...], (8, records))

    def rows_at(s):
        return jnp.where(
            row == s, box_b, jnp.where(row == 2 + s, elem_b, jnp.where(row == 4 + s, weight_b, 0.0))
        )

    tab = jnp.dot(
        rows_at(0), first, precision=lax.Precision.HIGHEST, preferred_element_type=F32
    ) + jnp.dot(
        rows_at(1), second, precision=lax.Precision.HIGHEST, preferred_element_type=F32
    )
    tab_f[...] = tab
    tab_i[...] = jnp.clip((tab + 0.25).astype(jnp.int32), 0, slots - 1)
    to_smem = [
        pltpu.make_async_copy(tab_f, sm_f, sm_sem.at[0]),
        pltpu.make_async_copy(tab_i, sm_i, sm_sem.at[1]),
    ]
    for copy in to_smem:
        copy.start()

    full = width // (2 * LANES) * 2 * LANES
    table[:, 0] = jnp.zeros((6, funcs, LANES), F32)
    small[11].wait()
    small[12].wait()
    for f in range(6):
        pad = jnp.zeros((LANES - trace, width), F32)
        value = jnp.concatenate([extract[OPPOSITE[f]], pad], axis=0)
        high, low = split(value.T)
        cols = slice(f * LANES, (f + 1) * LANES)
        pieces = [high[:full], high[:full], low[:full], high[full:], high[full:], low[full:]]
        if 3 * width < ext_cat.shape[0]:
            pieces += [jnp.zeros((ext_cat.shape[0] - 3 * width, LANES), BF16)]
        ext_cat[:, cols] = jnp.concatenate(pieces, axis=0)
        pad = jnp.zeros((LANES - trace, width), F32)
        high, low = split(jnp.concatenate([lift[f], pad], axis=0))
        lift_cat[0, f * LANES : (f + 1) * LANES] = high
        lift_cat[1, f * LANES : (f + 1) * LANES] = low

    small[6].wait()

    def spread(i, _):
        for k in range(8):
            for f in range(6):
                scale[f, i * 8 + k] = jnp.full((funcs, LANES), coef[f, i * 8 + k], F32)
        return 0

    lax.fori_loop(0, slots // 8, spread, 0)
    small[4].wait()
    small[5].wait()
    live = counts[0]
    batch = slots // 2

    def update(first_e, count, shade, source, first_step):
        fresh = []
        for k in range(count):
            value = source(first_e + k).astype(BF16)
            fresh.append(mm(value, dinv[first_e + k]))
        for k in range(count):
            e = first_e + k
            mask = jnp.where((colour[e] == shade) & (e < live), 1, 0)
            mask = jnp.full((funcs, width), mask, jnp.int32) > 0
            at = pl.ds(pl.multiple_of(e * funcs, funcs), funcs)
            old = jnp.zeros((funcs, width), F32) if first_step else psi[at]
            psi[at] = jnp.where(mask, fresh[k], old)

    small[10].wait()

    def start(i, _):
        span = pl.ds(i * chunk, chunk)
        pltpu.make_async_copy(dinv_hbm.at[span], dinv.at[span], dinv_sem.at[i]).wait()
        update(i * chunk, chunk, 0, lambda e: rhs[e], True)
        return 0

    lax.fori_loop(0, slots // chunk, start, 0)

    for i in (7, 8, 9, 13, 14):
        small[i].wait()
    pl.semaphore_wait(barrier, len(partners))
    def step_body(step, _):
        shade = lax.rem(step, 2)
        high, low = split(psi[...])
        pieces = [high[:, :full], low[:, :full], high[:, :full]]
        pieces += [high[:, full:], low[:, full:], high[:, full:]]
        if 3 * width < ext_cat.shape[0]:
            pieces += [jnp.zeros((rows, ext_cat.shape[0] - 3 * width), BF16)]
        state = jnp.concatenate(pieces, axis=1)

        def fill(pair):
            cols = pl.ds(pair * 2 * LANES, 2 * LANES)
            out = mm(state, ext_cat[:, cols])
            for half_ in range(2):
                table[pair * 2 + half_, 1 : slots + 1] = out[
                    :, half_ * LANES : (half_ + 1) * LANES
                ].reshape(slots, funcs, LANES)

        fill(0)
        for s in range(rim):
            out_up[step - 1, s] = table[0, send_hi[s] + 1]
            out_down[step - 1, s] = table[1, send_lo[s] + 1]
        up = pltpu.make_async_remote_copy(
            src_ref=out_up.at[step - 1],
            dst_ref=in_below.at[step - 1],
            send_sem=up_sem.at[0],
            recv_sem=up_sem.at[step],
            device_id=(above, fn),
            device_id_type=MESH,
        )
        up.start()
        down = pltpu.make_async_remote_copy(
            src_ref=out_down.at[step - 1],
            dst_ref=in_above.at[step - 1],
            send_sem=down_sem.at[0],
            recv_sem=down_sem.at[step],
            device_id=(below, fn),
            device_id_type=MESH,
        )
        down.start()

        @pl.when(step == 1)
        def _():
            homes = [
                (plane_peer(rd), near_first.index(back(rd))) for rd in near_first[1:]
            ]
            homes += [(place(x, column(j), y), A + opposite(j)) for j in range(Z - 1)]
            for peer, home in homes:
                pltpu.make_async_remote_copy(
                    src_ref=tab_f,
                    dst_ref=tabs_in.at[home],
                    send_sem=tab_sem.at[0],
                    recv_sem=tab_sem.at[1],
                    device_id=(peer, fn),
                    device_id_type=MESH,
                ).start()

        fill(1)
        fill(2)

        def gather(faces):
            def pairs(i, _):
                for f in faces:
                    found = []
                    for k in range(4):
                        e = i * 8 + k * 2
                        found.append(
                            jnp.concatenate(
                                [
                                    table[f, nbr[f, e] + 1] * scale[f, e],
                                    table[f, nbr[f, e + 1] + 1] * scale[f, e + 1],
                                ],
                                axis=0,
                            )
                        )
                    found = [split(value) for value in found]
                    for k in range(4):
                        start = pl.multiple_of((i * 8 + k * 2) * funcs, 2 * funcs)
                        at = pl.ds(start, 2 * funcs)
                        near_high[at, f * LANES : (f + 1) * LANES] = found[k][0]
                        near_low[at, f * LANES : (f + 1) * LANES] = found[k][1]
                return 0

            lax.fori_loop(0, slots // 8, pairs, 0)

        def lifted(lo, hi):
            a, b = lo * LANES, hi * LANES
            left = jnp.concatenate([near_high[:, a:b], near_low[:, a:b], near_high[:, a:b]], axis=1)
            right = jnp.concatenate([lift_cat[0, a:b], lift_cat[0, a:b], lift_cat[1, a:b]], axis=0)
            return mm(left, right)

        gather((2, 3, 4, 5))
        resid[...] = rhs[...].reshape(rows, width) - lifted(2, 6)
        up.wait_recv()
        down.wait_recv()
        table[0, slots + 1 : slots + 1 + rim] = in_below[step - 1]
        table[1, slots + 1 + rim : slots + 1 + 2 * rim] = in_above[step - 1]
        gather((0, 1))
        resid[...] = resid[...] - lifted(0, 2)

        def source(e):
            return resid[pl.ds(pl.multiple_of(e * funcs, funcs), funcs)]

        def sweep(i, _):
            update(i * batch, batch, shade, source, False)
            return 0

        lax.fori_loop(0, slots // batch, sweep, 0)
        up.wait_send()
        down.wait_send()
        return 0

    lax.fori_loop(1, 2 * SWEEPS, step_body, 0)

    high, low = split(psi[...])
    sensed[...] = (mm(high, wall_map[...]) + mm(low, wall_map[...])).reshape(
        slots, funcs, LANES
    )
    for copy in to_smem:
        copy.wait()

    def slot(owner, which):
        return sensed[sm_i[2 + which, owner]] * sm_f[4 + which, owner]

    for j in range(Z):
        for d, rd in enumerate(far_first):
            px, py = lax.rem(x + rd // Y, X), lax.rem(y + rd % Y, Y)
            for which in range(2):
                far_send[j, d, which] = slot(place(px, column(j), py), which)
        if j < Z - 1:
            pltpu.make_async_remote_copy(
                src_ref=far_send.at[j],
                dst_ref=far_recv.at[opposite(j)],
                send_sem=far_sem.at[0],
                recv_sem=far_sem.at[1],
                device_id=(place(x, column(j), y), fn),
                device_id_type=MESH,
            ).start()
    per = rec_sem.shape[0] - 1
    group = Z // per

    def send_near(c):
        span = pl.ds(c * group, group)
        for a, rd in enumerate(near_first):
            px, py = lax.rem(x + rd // Y, X), lax.rem(y + rd % Y, Y)
            for j in range(c * group, (c + 1) * group):
                for which in range(2):
                    send_rec[a, j, which] = slot(place(px, column(j), py), which)
            if a:
                pltpu.make_async_remote_copy(
                    src_ref=send_rec.at[a, span],
                    dst_ref=recv_rec.at[near_first.index(back(rd)), span],
                    send_sem=rec_sem.at[per],
                    recv_sem=rec_sem.at[c],
                    device_id=(plane_peer(rd), fn),
                    device_id_type=MESH,
                ).start()

    for c in range(per):
        send_near(c)
    wait_for(tabs_in.at[1 : A + Z - 1], tab_sem.at[1])
    tabs_in[0] = tab_f[...]
    tabs_in[A + Z - 1] = tab_f[...]
    boxes_i[...] = (tabs_in[...] + 0.25).astype(jnp.int32)
    boxes = pltpu.make_async_copy(boxes_i, sm_boxes, sm_sem.at[2])
    boxes.start()
    boxes.wait()

    sub_f = lax.broadcasted_iota(jnp.int32, (funcs, LANES), 0)
    weight = jnp.zeros((funcs, LANES), F32)
    for j in range(funcs):
        weight = jnp.where(sub_f == j, fweights[j], weight)
    none = (jnp.zeros((funcs, LANES), F32),) * BOX_DEV

    def add(value, box, total):
        which = jnp.full((funcs, LANES), box, jnp.int32)
        return tuple(t + jnp.where(which == b, value, 0.0) for b, t in enumerate(total))

    def weighted(total):
        return jnp.concatenate(
            [jnp.sum(total[b] * weight, axis=0, keepdims=True) for b in range(BOX_DEV)], axis=0
        )

    def hand_on(total, full, summed, at, full_in, summed_in, home, peer, sems):
        for b in range(BOX_DEV):
            full[at, b] = total[b]
        summed[at] = weighted(total)
        pltpu.make_async_remote_copy(
            src_ref=summed.at[at],
            dst_ref=summed_in.at[home],
            send_sem=sems.at[2],
            recv_sem=sems.at[3],
            device_id=(peer, 1 - fn),
            device_id_type=MESH,
        ).start()
        pltpu.make_async_remote_copy(
            src_ref=full.at[at],
            dst_ref=full_in.at[home],
            send_sem=sems.at[0],
            recv_sem=sems.at[1],
            device_id=(peer, fn),
            device_id_type=MESH,
        ).start()

    def near_sums(c):
        wait_for(recv_rec.at[1:, pl.ds(c * group, group)], rec_sem.at[c])
        for j in range(c * group, (c + 1) * group):
            owner = place(x, column(j), y)
            total = none
            for s in range(2):
                total = add(send_rec[0, j, s], sm_boxes[0, s, owner], total)

            def accumulate(a, total):
                for s in range(2):
                    total = add(recv_rec[a, j, s], sm_boxes[a, s, owner], total)
                return total

            total = lax.fori_loop(1, A, accumulate, total)
            if j < Z - 1:
                peer = place(x, column(j), y)
                hand_on(total, z_send, part, j, z_recv, part_in, opposite(j), peer, z_sem)
            else:
                for b in range(BOX_DEV):
                    z_send[j, b] = total[b]
                part[j] = weighted(total)
                pltpu.make_async_remote_copy(
                    src_ref=part.at[j],
                    dst_ref=part_in.at[j],
                    send_sem=z_sem.at[2],
                    recv_sem=z_sem.at[3],
                    device_id=(me, 1 - fn),
                    device_id_type=MESH,
                ).start()

    def far_sums():
        wait_for(far_recv.at[: Z - 1], far_sem.at[1])
        for d, rd in enumerate(far_first):
            px, py = lax.rem(x + rd // Y, X), lax.rem(y + rd % Y, Y)
            owner = place(px, z, py)
            total = none
            for s in range(2):
                total = add(far_send[Z - 1, d, s], sm_boxes[A + Z - 1, s, owner], total)

            def accumulate(j, total):
                for s in range(2):
                    total = add(far_recv[j, d, s], sm_boxes[A + j, s, owner], total)
                return total

            total = lax.fori_loop(0, Z - 1, accumulate, total)
            home = far_first.index(back(rd))
            hand_on(
                total, last_send, last_part, d, last_recv, last_part_in, home, owner, last_sem
            )

    for c in range(per):
        near_sums(c)
        if c == per // 2 - 1:
            far_sums()

    result = z_send[Z - 1]
    wait_for(z_recv.at[: Z - 1], z_sem.at[1])
    wait_for(part_in, z_sem.at[3])
    own_part = part_in[Z - 1]
    for j in range(Z - 1):
        result = result + z_recv[j]
        own_part = own_part + part_in[j]
    wait_for(last_recv, last_sem.at[1])
    wait_for(last_part_in, last_sem.at[3])
    for d in range(B):
        result = result + last_recv[d]
        own_part = own_part + last_part_in[d]
    grad[...] = result
    combined[...] = own_part + jnp.sum(result * weight[None], axis=1)

    wait_for(tabs_in.at[1 : A + Z - 1], tab_sem.at[0])
    wait_for(send_rec.at[1:], rec_sem.at[per])
    wait_for(z_send.at[: Z - 1], z_sem.at[0])
    wait_for(part, z_sem.at[2])
    wait_for(far_send.at[: Z - 1], far_sem.at[0])
    wait_for(last_send, last_sem.at[0])
    wait_for(last_part, last_sem.at[2])


def body(
    rhs,
    dinv,
    extract,
    lift,
    coef,
    nbr,
    colour,
    counts,
    send_lo,
    send_hi,
    rec_elem,
    rec_owner,
    rec_box,
    rec_weight,
    wall_map,
    fweights,
):
    slots, funcs, width = rhs.shape
    rim = send_lo.shape[0]
    records = rec_elem.shape[0]
    owners = lax.axis_size("dom")
    X, Z, Y = GRIDS[owners]
    rows = slots * funcs
    steps = 2 * SWEEPS - 1
    blocks = 8
    per = min(4, Z)
    B = len(far_displacements(X, Y))
    A = X * Y - B
    hbm = pl.BlockSpec(memory_space=pltpu.HBM)
    vmem = pl.BlockSpec(memory_space=pltpu.VMEM)
    dma = pltpu.SemaphoreType.DMA
    sums = pl.pallas_call(
        functools.partial(kernel, (X, Z, Y)),
        out_shape=(
            jax.ShapeDtypeStruct((BOX_DEV, funcs, LANES), F32),
            jax.ShapeDtypeStruct((BOX_DEV, LANES), F32),
        ),
        in_specs=[hbm] * 16,
        out_specs=(vmem, vmem),
        scratch_shapes=[
            pltpu.VMEM(rhs.shape, F32),
            pltpu.VMEM(dinv.shape, BF16),
            pltpu.VMEM(lift.shape, F32),
            pltpu.VMEM(lift.shape, F32),
            pltpu.SMEM((6, slots), F32),
            pltpu.SMEM((6, slots), jnp.int32),
            pltpu.SMEM((slots,), jnp.int32),
            pltpu.SMEM((1,), jnp.int32),
            pltpu.SMEM((rim,), jnp.int32),
            pltpu.SMEM((rim,), jnp.int32),
            pltpu.VMEM((1, records), jnp.int32),
            pltpu.VMEM((1, records), jnp.int32),
            pltpu.VMEM((1, records), jnp.int32),
            pltpu.VMEM((1, records), F32),
            pltpu.VMEM(wall_map.shape, BF16),
            pltpu.SMEM((funcs,), F32),
            pltpu.VMEM((pl.cdiv(3 * width, 2 * LANES) * 2 * LANES, 6 * LANES), BF16),
            pltpu.VMEM((2, 6 * LANES, width), BF16),
            pltpu.VMEM((rows, width), F32),
            pltpu.VMEM((6, slots + 2 * rim + 1, funcs, LANES), F32),
            pltpu.VMEM((6, slots, funcs, LANES), F32),
            pltpu.VMEM((rows, 6 * LANES), BF16),
            pltpu.VMEM((rows, 6 * LANES), BF16),
            pltpu.VMEM((rows, width), F32),
            pltpu.VMEM((slots, funcs, LANES), F32),
            pltpu.VMEM((steps, rim, funcs, LANES), F32),
            pltpu.VMEM((steps, rim, funcs, LANES), F32),
            pltpu.VMEM((steps, rim, funcs, LANES), F32),
            pltpu.VMEM((steps, rim, funcs, LANES), F32),
            pltpu.VMEM((8, owners), F32),
            pltpu.VMEM((8, owners), jnp.int32),
            pltpu.SMEM((8, owners), F32),
            pltpu.SMEM((8, owners), jnp.int32),
            pltpu.VMEM((A + Z, 8, owners), F32),
            pltpu.VMEM((A + Z, 8, owners), jnp.int32),
            pltpu.SMEM((A + Z, 8, owners), jnp.int32),
            pltpu.VMEM((A, Z, 2, funcs, LANES), F32),
            pltpu.VMEM((A, Z, 2, funcs, LANES), F32),
            pltpu.VMEM((Z, BOX_DEV, funcs, LANES), F32),
            pltpu.VMEM((Z, BOX_DEV, funcs, LANES), F32),
            pltpu.VMEM((Z, BOX_DEV, LANES), F32),
            pltpu.VMEM((Z, BOX_DEV, LANES), F32),
            pltpu.VMEM((Z, B, 2, funcs, LANES), F32),
            pltpu.VMEM((Z, B, 2, funcs, LANES), F32),
            pltpu.VMEM((B, BOX_DEV, funcs, LANES), F32),
            pltpu.VMEM((B, BOX_DEV, funcs, LANES), F32),
            pltpu.VMEM((B, BOX_DEV, LANES), F32),
            pltpu.VMEM((B, BOX_DEV, LANES), F32),
            dma((15,)),
            dma((blocks,)),
            dma((3,)),
            dma((1 + steps,)),
            dma((1 + steps,)),
            dma((2,)),
            dma((per + 1,)),
            dma((4,)),
            dma((2,)),
            dma((4,)),
        ],
        compiler_params=pltpu.CompilerParams(
            collective_id=0, has_side_effects=True, vmem_limit_bytes=64 * 1024 * 1024
        ),
    )(
        rhs,
        dinv,
        extract.transpose(0, 2, 1),
        lift,
        coef.T,
        nbr.T,
        colour,
        counts,
        send_lo,
        send_hi,
        rec_elem.reshape(1, records),
        rec_owner.T,
        rec_box.reshape(1, records),
        rec_weight.reshape(1, records),
        wall_map,
        fweights,
    )
    return pl.pallas_call(
        hand_over,
        out_shape=(
            jax.ShapeDtypeStruct((BOX_DEV, funcs, LANES), F32),
            jax.ShapeDtypeStruct((BOX_DEV, LANES), F32),
        ),
        in_specs=[hbm] * 2,
        out_specs=(hbm, hbm),
        scratch_shapes=[dma((2,))],
        compiler_params=pltpu.CompilerParams(vmem_limit_bytes=64 * 1024 * 1024),
    )(*sums)


def solution(mesh):
    placed = (
        P("dom", "fn", None),
        P("dom", None, None),
        P(),
        P(),
        P("dom", None),
        P("dom", None),
        P("dom"),
        P("dom"),
        P("dom"),
        P("dom"),
        P("dom"),
        P("dom", None),
        P("dom"),
        P("dom"),
        P(),
        P("fn"),
    )
    return jax.shard_map(
        body,
        mesh=mesh,
        in_specs=placed,
        out_specs=(P("dom", "fn", None), P("dom", None)),
        check_vma=False,
    )
```

```python
import functools
import jax
import jax.numpy as jnp
from jax import lax
from jax.experimental import pallas as pl
from jax.experimental.pallas import tpu as pltpu
from jax.sharding import PartitionSpec as P

BOX_DEV = 4
SWEEPS = 2
OPPOSITE = (1, 0, 3, 2, 5, 4)
LANES = 128
GRIDS = {128: (4, 8, 4), 8: (2, 2, 2)}
MESH = pl.DeviceIdType.MESH
F32 = jnp.float32
BF16 = jnp.bfloat16


def split(value):
    high = value.astype(BF16)
    return high, (value - high.astype(F32)).astype(BF16)


def mm(a, b):
    return jnp.dot(a, b, preferred_element_type=F32)


def far_displacements(X, Y):
    def hops(rd):
        dx, dy = rd // Y, rd % Y
        return min(dx, X - dx) + min(dy, Y - dy)

    longest = 3 if X == 4 else 2
    return [rd for rd in range(X * Y) if hops(rd) == longest]


def hand_over(grad_in, combined_in, grad, combined, sem):
    copies = [
        pltpu.make_async_copy(grad_in, grad, sem.at[0]),
        pltpu.make_async_copy(combined_in, combined, sem.at[1]),
    ]
    for copy in copies:
        copy.start()
    for copy in copies:
        copy.wait()


def kernel(
    dims,
    rhs_hbm,
    dinv_hbm,
    extract_hbm,
    lift_hbm,
    coef_hbm,
    nbr_hbm,
    colour_hbm,
    counts_hbm,
    send_lo_hbm,
    send_hi_hbm,
    rec_elem_hbm,
    rec_owner_hbm,
    rec_box_hbm,
    rec_weight_hbm,
    wall_map_hbm,
    fweights_hbm,
    grad,
    combined,
    rhs,
    dinv,
    extract,
    lift,
    coef,
    nbr,
    colour,
    counts,
    send_lo,
    send_hi,
    rec_elem,
    rec_owner,
    rec_box,
    rec_weight,
    wall_map,
    fweights,
    ext_cat,
    lift_cat,
    psi,
    table,
    scale,
    near_high,
    near_low,
    resid,
    sensed,
    out_up,
    out_down,
    in_below,
    in_above,
    tab_f,
    tab_i,
    sm_f,
    sm_i,
    tabs_in,
    boxes_i,
    sm_boxes,
    send_rec,
    recv_rec,
    z_send,
    z_recv,
    part,
    part_in,
    far_send,
    far_recv,
    last_send,
    last_recv,
    last_part,
    last_part_in,
    load_sem,
    dinv_sem,
    sm_sem,
    up_sem,
    down_sem,
    tab_sem,
    rec_sem,
    z_sem,
    far_sem,
    last_sem,
):
    X, Z, Y = dims
    XY = X * Y
    slots, funcs, width = rhs.shape
    rows = slots * funcs
    trace = extract.shape[1]
    rim = out_up.shape[1]
    records = rec_elem.shape[1]
    owners = X * Z * Y
    chunk = slots // dinv_sem.shape[0]
    me = lax.axis_index("dom")
    fn = lax.axis_index("fn")
    x = me // (Z * Y)
    z = (me // Y) % Z
    y = me % Y
    above = lax.rem(me + 1, owners)
    below = lax.rem(me + owners - 1, owners)

    def place(px, pz, py):
        return (px * Z + pz) * Y + py

    def plane_peer(rd):
        dx, dy = rd // Y, rd % Y
        return place(lax.rem(x + dx, X), z, lax.rem(y + dy, Y))

    def wait_for(ref, sem):
        pltpu.make_async_copy(ref, ref, sem).wait()

    def back(rd):
        dx, dy = rd // Y, rd % Y
        return ((X - dx) % X) * Y + (Y - dy) % Y

    far_first = far_displacements(X, Y)
    near_first = [rd for rd in range(XY) if rd not in far_first]
    A, B = len(near_first), len(far_first)

    half = Z // 2
    shifts = [half]
    for step in range(1, half):
        shifts += [half - step, half + step]
    shifts += [0]

    def column(j):
        return lax.rem(z + shifts[j], Z)

    def opposite(j):
        return shifts.index((Z - shifts[j]) % Z)

    order = (
        (rec_owner_hbm, rec_owner),
        (rec_elem_hbm, rec_elem),
        (rec_box_hbm, rec_box),
        (rec_weight_hbm, rec_weight),
        (colour_hbm, colour),
        (counts_hbm, counts),
        (coef_hbm, coef),
        (nbr_hbm, nbr),
        (send_lo_hbm, send_lo),
        (send_hi_hbm, send_hi),
        (rhs_hbm, rhs),
        (extract_hbm, extract),
        (lift_hbm, lift),
        (wall_map_hbm, wall_map),
        (fweights_hbm, fweights),
    )
    small = []
    for i, (src, dst) in enumerate(order):
        copy = pltpu.make_async_copy(src, dst, load_sem.at[i])
        copy.start()
        small.append(copy)
    chunks = slots // chunk

    def block(i):
        span = pl.ds(i * chunk, chunk)
        return pltpu.make_async_copy(dinv_hbm.at[span], dinv.at[span], dinv_sem.at[i])

    ahead = 3
    for i in range(ahead):
        block(i).start()

    barrier = pltpu.get_barrier_semaphore()
    partners = [(above, fn), (below, fn), (me, 1 - fn)]
    partners += [(plane_peer(rd), fn) for rd in range(1, XY)]
    partners += [(plane_peer(rd), 1 - fn) for rd in far_first]
    partners += [(place(x, column(j), y), fn) for j in range(Z - 1)]
    partners += [(place(x, column(j), y), 1 - fn) for j in range(Z - 1)]
    for partner in partners:
        pl.semaphore_signal(barrier, inc=1, device_id=partner, device_id_type=MESH)

    for copy in small[:4]:
        copy.wait()
    lane = lax.broadcasted_iota(jnp.int32, (records, records), 1)
    sub = lax.broadcasted_iota(jnp.int32, (records, records), 0)
    own = jnp.broadcast_to(rec_owner[...], (records, records)).astype(F32)
    own_col = jnp.sum(jnp.where(lane == sub, own, 0.0), axis=1, keepdims=True)
    same = (own == own_col) & (lane < sub)
    rank = jnp.sum(jnp.where(same, 1.0, 0.0), axis=1, keepdims=True)
    lane_o = lax.broadcasted_iota(jnp.int32, (records, owners), 1).astype(F32)
    first = jnp.where((own_col == lane_o) & (rank < 0.5), 1.0, 0.0)
    second = jnp.where((own_col == lane_o) & (rank > 0.5), 1.0, 0.0)
    row = lax.broadcasted_iota(jnp.int32, (8, records), 0)
    elem_b = jnp.broadcast_to(rec_elem[...].astype(F32), (8, records))
    box_b = jnp.broadcast_to(rec_box[...].astype(F32), (8, records))
    weight_b = jnp.broadcast_to(rec_weight[...], (8, records))

    def rows_at(s):
        return jnp.where(
            row == s, box_b, jnp.where(row == 2 + s, elem_b, jnp.where(row == 4 + s, weight_b, 0.0))
        )

    tab = jnp.dot(
        rows_at(0), first, precision=lax.Precision.HIGHEST, preferred_element_type=F32
    ) + jnp.dot(
        rows_at(1), second, precision=lax.Precision.HIGHEST, preferred_element_type=F32
    )
    tab_f[...] = tab
    tab_i[...] = jnp.clip((tab + 0.25).astype(jnp.int32), 0, slots - 1)
    to_smem = [
        pltpu.make_async_copy(tab_f, sm_f, sm_sem.at[0]),
        pltpu.make_async_copy(tab_i, sm_i, sm_sem.at[1]),
    ]
    for copy in to_smem:
        copy.start()

    full = width // (2 * LANES) * 2 * LANES
    table[:, 0] = jnp.zeros((6, funcs, LANES), F32)
    small[11].wait()
    small[12].wait()
    for f in range(6):
        pad = jnp.zeros((LANES - trace, width), F32)
        value = jnp.concatenate([extract[OPPOSITE[f]], pad], axis=0)
        high, low = split(value.T)
        cols = slice(f * LANES, (f + 1) * LANES)
        pieces = [high[:full], high[:full], low[:full], high[full:], high[full:], low[full:]]
        if 3 * width < ext_cat.shape[0]:
            pieces += [jnp.zeros((ext_cat.shape[0] - 3 * width, LANES), BF16)]
        ext_cat[:, cols] = jnp.concatenate(pieces, axis=0)
        pad = jnp.zeros((LANES - trace, width), F32)
        high, low = split(jnp.concatenate([lift[f], pad], axis=0))
        lift_cat[0, f * LANES : (f + 1) * LANES] = high
        lift_cat[1, f * LANES : (f + 1) * LANES] = low

    small[6].wait()

    def spread(i, _):
        for k in range(8):
            for f in range(6):
                scale[f, i * 8 + k] = jnp.full((funcs, LANES), coef[f, i * 8 + k], F32)
        return 0

    lax.fori_loop(0, slots // 8, spread, 0)
    small[4].wait()
    small[5].wait()
    live = counts[0]
    batch = slots // 2

    def chosen(e, shade):
        mask = jnp.where((colour[e] == shade) & (e < live), 1, 0)
        return jnp.full((funcs, width), mask, jnp.int32) > 0

    def update(first_e, count, shade, source, first_step):
        fresh = []
        for k in range(count):
            value = source(first_e + k).astype(BF16)
            fresh.append(mm(value, dinv[first_e + k]))
        for k in range(count):
            e = first_e + k
            old = jnp.zeros((funcs, width), F32) if first_step else psi[e]
            psi[e] = jnp.where(chosen(e, shade), fresh[k], old)

    def terms(value):
        high, low = split(value)
        pieces = [high[:, :full], low[:, :full], high[:, :full]]
        pieces += [high[:, full:], low[:, full:], high[:, full:]]
        if 3 * width < ext_cat.shape[0]:
            pieces += [jnp.zeros((value.shape[0], ext_cat.shape[0] - 3 * width), BF16)]
        return jnp.concatenate(pieces, axis=1)

    def fill(first_e, count):
        span = pl.ds(first_e, count)
        out = mm(terms(psi[span].reshape(count * funcs, width)), ext_cat[...])
        for f in range(6):
            table[f, pl.ds(first_e + 1, count)] = out[:, f * LANES : (f + 1) * LANES].reshape(
                count, funcs, LANES
            )

    small[10].wait()

    def start(i, _):
        block(i).wait()

        @pl.when(i + ahead < chunks)
        def _():
            block(i + ahead).start()

        update(i * chunk, chunk, 0, lambda e: rhs[e], True)
        return 0

    lax.fori_loop(0, chunks, start, 0)
    for i in (7, 8, 9, 13, 14):
        small[i].wait()
    pl.semaphore_wait(barrier, len(partners))
    def chain(index):
        up = pltpu.make_async_remote_copy(
            src_ref=out_up.at[index],
            dst_ref=in_below.at[index],
            send_sem=up_sem.at[0],
            recv_sem=up_sem.at[1 + index],
            device_id=(above, fn),
            device_id_type=MESH,
        )
        down = pltpu.make_async_remote_copy(
            src_ref=out_down.at[index],
            dst_ref=in_above.at[index],
            send_sem=down_sem.at[0],
            recv_sem=down_sem.at[1 + index],
            device_id=(below, fn),
            device_id_type=MESH,
        )
        return up, down

    def export(index, away):
        out = mm(terms(jnp.concatenate(away, axis=0)), ext_cat[:, : 2 * LANES])
        count = rim * funcs
        out_up[index] = out[:count, :LANES].reshape(rim, funcs, LANES)
        out_down[index] = out[count:, LANES:].reshape(rim, funcs, LANES)
        for copy in chain(index):
            copy.start()

    listed = [send_hi[s] for s in range(rim)] + [send_lo[s] for s in range(rim)]
    export(0, [psi[e] for e in listed])

    def step_body(step, _):
        shade = lax.rem(step, 2)

        @pl.when(step == 2)
        def _():
            homes = [
                (plane_peer(rd), near_first.index(back(rd))) for rd in near_first[1:]
            ]
            homes += [(place(x, column(j), y), A + opposite(j)) for j in range(Z - 1)]
            for peer, home in homes:
                pltpu.make_async_remote_copy(
                    src_ref=tab_f,
                    dst_ref=tabs_in.at[home],
                    send_sem=tab_sem.at[0],
                    recv_sem=tab_sem.at[1],
                    device_id=(peer, fn),
                    device_id_type=MESH,
                ).start()

        @pl.when(step > 0)
        def _():
            fill(0, slots)

        def gather(faces):
            def pairs(i, _):
                for f in faces:
                    found = []
                    for k in range(4):
                        e = i * 8 + k * 2
                        found.append(
                            jnp.concatenate(
                                [
                                    table[f, nbr[f, e] + 1] * scale[f, e],
                                    table[f, nbr[f, e + 1] + 1] * scale[f, e + 1],
                                ],
                                axis=0,
                            )
                        )
                    found = [split(value) for value in found]
                    for k in range(4):
                        start = pl.multiple_of((i * 8 + k * 2) * funcs, 2 * funcs)
                        at = pl.ds(start, 2 * funcs)
                        near_high[at, f * LANES : (f + 1) * LANES] = found[k][0]
                        near_low[at, f * LANES : (f + 1) * LANES] = found[k][1]
                return 0

            lax.fori_loop(0, slots // 8, pairs, 0)

        def lifted(lo, hi):
            a, b = lo * LANES, hi * LANES
            left = jnp.concatenate([near_high[:, a:b], near_low[:, a:b], near_high[:, a:b]], axis=1)
            right = jnp.concatenate([lift_cat[0, a:b], lift_cat[0, a:b], lift_cat[1, a:b]], axis=0)
            return mm(left, right)

        gather((2, 3, 4, 5))
        resid[...] = rhs[...] - lifted(2, 6).reshape(slots, funcs, width)
        for copy in chain(step - 1):
            copy.wait_recv()
        table[0, slots + 1 : slots + 1 + rim] = in_below[step - 1]
        table[1, slots + 1 + rim : slots + 1 + 2 * rim] = in_above[step - 1]
        gather((0, 1))
        resid[...] = resid[...] - lifted(0, 2).reshape(slots, funcs, width)

        @pl.when(step < 2 * SWEEPS - 1)
        def _():
            fresh = [mm(resid[e].astype(BF16), dinv[e]) for e in listed]
            export(
                step, [jnp.where(chosen(e, shade), new, psi[e]) for e, new in zip(listed, fresh)]
            )

        def sweep(i, _):
            update(i * batch, batch, shade, lambda e: resid[e], False)
            return 0

        lax.fori_loop(0, slots // batch, sweep, 0)
        return 0

    lax.fori_loop(1, 2 * SWEEPS, step_body, 0)

    high, low = split(psi[...].reshape(rows, width))
    sensed[...] = (mm(high, wall_map[...]) + mm(low, wall_map[...])).reshape(
        slots, funcs, LANES
    )
    for copy in to_smem:
        copy.wait()

    def slot(owner, which):
        return sensed[sm_i[2 + which, owner]] * sm_f[4 + which, owner]

    for j in range(Z):
        for d, rd in enumerate(far_first):
            px, py = lax.rem(x + rd // Y, X), lax.rem(y + rd % Y, Y)
            for which in range(2):
                far_send[j, d, which] = slot(place(px, column(j), py), which)
        if j < Z - 1:
            pltpu.make_async_remote_copy(
                src_ref=far_send.at[j],
                dst_ref=far_recv.at[opposite(j)],
                send_sem=far_sem.at[0],
                recv_sem=far_sem.at[1],
                device_id=(place(x, column(j), y), fn),
                device_id_type=MESH,
            ).start()
    per = rec_sem.shape[0] - 1
    group = Z // per

    def send_near(c):
        span = pl.ds(c * group, group)
        for a, rd in enumerate(near_first):
            px, py = lax.rem(x + rd // Y, X), lax.rem(y + rd % Y, Y)
            for j in range(c * group, (c + 1) * group):
                for which in range(2):
                    send_rec[a, j, which] = slot(place(px, column(j), py), which)
            if a:
                pltpu.make_async_remote_copy(
                    src_ref=send_rec.at[a, span],
                    dst_ref=recv_rec.at[near_first.index(back(rd)), span],
                    send_sem=rec_sem.at[per],
                    recv_sem=rec_sem.at[c],
                    device_id=(plane_peer(rd), fn),
                    device_id_type=MESH,
                ).start()

    for c in range(per):
        send_near(c)
    wait_for(tabs_in.at[1 : A + Z - 1], tab_sem.at[1])
    tabs_in[0] = tab_f[...]
    tabs_in[A + Z - 1] = tab_f[...]
    boxes_i[...] = (tabs_in[...] + 0.25).astype(jnp.int32)
    boxes = pltpu.make_async_copy(boxes_i, sm_boxes, sm_sem.at[2])
    boxes.start()
    boxes.wait()

    sub_f = lax.broadcasted_iota(jnp.int32, (funcs, LANES), 0)
    weight = jnp.zeros((funcs, LANES), F32)
    for j in range(funcs):
        weight = jnp.where(sub_f == j, fweights[j], weight)
    none = (jnp.zeros((funcs, LANES), F32),) * BOX_DEV

    def add(value, box, total):
        which = jnp.full((funcs, LANES), box, jnp.int32)
        return tuple(t + jnp.where(which == b, value, 0.0) for b, t in enumerate(total))

    def weighted(total):
        return jnp.concatenate(
            [jnp.sum(total[b] * weight, axis=0, keepdims=True) for b in range(BOX_DEV)], axis=0
        )

    def hand_on(total, full, summed, at, full_in, summed_in, home, peer, sems):
        for b in range(BOX_DEV):
            full[at, b] = total[b]
        summed[at] = weighted(total)
        pltpu.make_async_remote_copy(
            src_ref=summed.at[at],
            dst_ref=summed_in.at[home],
            send_sem=sems.at[2],
            recv_sem=sems.at[3],
            device_id=(peer, 1 - fn),
            device_id_type=MESH,
        ).start()
        pltpu.make_async_remote_copy(
            src_ref=full.at[at],
            dst_ref=full_in.at[home],
            send_sem=sems.at[0],
            recv_sem=sems.at[1],
            device_id=(peer, fn),
            device_id_type=MESH,
        ).start()

    def near_sums(c):
        wait_for(recv_rec.at[1:, pl.ds(c * group, group)], rec_sem.at[c])
        for j in range(c * group, (c + 1) * group):
            owner = place(x, column(j), y)
            total = none
            for s in range(2):
                total = add(send_rec[0, j, s], sm_boxes[0, s, owner], total)

            def accumulate(a, total):
                for s in range(2):
                    total = add(recv_rec[a, j, s], sm_boxes[a, s, owner], total)
                return total

            total = lax.fori_loop(1, A, accumulate, total)
            if j < Z - 1:
                peer = place(x, column(j), y)
                hand_on(total, z_send, part, j, z_recv, part_in, opposite(j), peer, z_sem)
            else:
                for b in range(BOX_DEV):
                    z_send[j, b] = total[b]
                part[j] = weighted(total)
                pltpu.make_async_remote_copy(
                    src_ref=part.at[j],
                    dst_ref=part_in.at[j],
                    send_sem=z_sem.at[2],
                    recv_sem=z_sem.at[3],
                    device_id=(me, 1 - fn),
                    device_id_type=MESH,
                ).start()

    def far_sums():
        wait_for(far_recv.at[: Z - 1], far_sem.at[1])
        for d, rd in enumerate(far_first):
            px, py = lax.rem(x + rd // Y, X), lax.rem(y + rd % Y, Y)
            owner = place(px, z, py)
            total = none
            for s in range(2):
                total = add(far_send[Z - 1, d, s], sm_boxes[A + Z - 1, s, owner], total)

            def accumulate(j, total):
                for s in range(2):
                    total = add(far_recv[j, d, s], sm_boxes[A + j, s, owner], total)
                return total

            total = lax.fori_loop(0, Z - 1, accumulate, total)
            home = far_first.index(back(rd))
            hand_on(
                total, last_send, last_part, d, last_recv, last_part_in, home, owner, last_sem
            )

    for c in range(per):
        near_sums(c)
        if c == per // 2 - 1:
            far_sums()

    result = z_send[Z - 1]
    wait_for(z_recv.at[: Z - 1], z_sem.at[1])
    wait_for(part_in, z_sem.at[3])
    own_part = part_in[Z - 1]
    for j in range(Z - 1):
        result = result + z_recv[j]
        own_part = own_part + part_in[j]
    wait_for(last_recv, last_sem.at[1])
    wait_for(last_part_in, last_sem.at[3])
    for d in range(B):
        result = result + last_recv[d]
        own_part = own_part + last_part_in[d]
    grad[...] = result
    combined[...] = own_part + jnp.sum(result * weight[None], axis=1)

    wait_for(out_up, up_sem.at[0])
    wait_for(out_down, down_sem.at[0])
    wait_for(tabs_in.at[1 : A + Z - 1], tab_sem.at[0])
    wait_for(send_rec.at[1:], rec_sem.at[per])
    wait_for(z_send.at[: Z - 1], z_sem.at[0])
    wait_for(part, z_sem.at[2])
    wait_for(far_send.at[: Z - 1], far_sem.at[0])
    wait_for(last_send, last_sem.at[0])
    wait_for(last_part, last_sem.at[2])


def body(
    rhs,
    dinv,
    extract,
    lift,
    coef,
    nbr,
    colour,
    counts,
    send_lo,
    send_hi,
    rec_elem,
    rec_owner,
    rec_box,
    rec_weight,
    wall_map,
    fweights,
):
    slots, funcs, width = rhs.shape
    rim = send_lo.shape[0]
    records = rec_elem.shape[0]
    owners = lax.axis_size("dom")
    X, Z, Y = GRIDS[owners]
    rows = slots * funcs
    steps = 2 * SWEEPS - 1
    blocks = 8
    per = min(4, Z)
    B = len(far_displacements(X, Y))
    A = X * Y - B
    hbm = pl.BlockSpec(memory_space=pltpu.HBM)
    vmem = pl.BlockSpec(memory_space=pltpu.VMEM)
    dma = pltpu.SemaphoreType.DMA
    sums = pl.pallas_call(
        functools.partial(kernel, (X, Z, Y)),
        out_shape=(
            jax.ShapeDtypeStruct((BOX_DEV, funcs, LANES), F32),
            jax.ShapeDtypeStruct((BOX_DEV, LANES), F32),
        ),
        in_specs=[hbm] * 16,
        out_specs=(vmem, vmem),
        scratch_shapes=[
            pltpu.VMEM(rhs.shape, F32),
            pltpu.VMEM(dinv.shape, BF16),
            pltpu.VMEM(lift.shape, F32),
            pltpu.VMEM(lift.shape, F32),
            pltpu.SMEM((6, slots), F32),
            pltpu.SMEM((6, slots), jnp.int32),
            pltpu.SMEM((slots,), jnp.int32),
            pltpu.SMEM((1,), jnp.int32),
            pltpu.SMEM((rim,), jnp.int32),
            pltpu.SMEM((rim,), jnp.int32),
            pltpu.VMEM((1, records), jnp.int32),
            pltpu.VMEM((1, records), jnp.int32),
            pltpu.VMEM((1, records), jnp.int32),
            pltpu.VMEM((1, records), F32),
            pltpu.VMEM(wall_map.shape, BF16),
            pltpu.SMEM((funcs,), F32),
            pltpu.VMEM((pl.cdiv(3 * width, 2 * LANES) * 2 * LANES, 6 * LANES), BF16),
            pltpu.VMEM((2, 6 * LANES, width), BF16),
            pltpu.VMEM((slots, funcs, width), F32),
            pltpu.VMEM((6, slots + 2 * rim + 1, funcs, LANES), F32),
            pltpu.VMEM((6, slots, funcs, LANES), F32),
            pltpu.VMEM((rows, 6 * LANES), BF16),
            pltpu.VMEM((rows, 6 * LANES), BF16),
            pltpu.VMEM((slots, funcs, width), F32),
            pltpu.VMEM((slots, funcs, LANES), F32),
            pltpu.VMEM((steps, rim, funcs, LANES), F32),
            pltpu.VMEM((steps, rim, funcs, LANES), F32),
            pltpu.VMEM((steps, rim, funcs, LANES), F32),
            pltpu.VMEM((steps, rim, funcs, LANES), F32),
            pltpu.VMEM((8, owners), F32),
            pltpu.VMEM((8, owners), jnp.int32),
            pltpu.SMEM((8, owners), F32),
            pltpu.SMEM((8, owners), jnp.int32),
            pltpu.VMEM((A + Z, 8, owners), F32),
            pltpu.VMEM((A + Z, 8, owners), jnp.int32),
            pltpu.SMEM((A + Z, 8, owners), jnp.int32),
            pltpu.VMEM((A, Z, 2, funcs, LANES), F32),
            pltpu.VMEM((A, Z, 2, funcs, LANES), F32),
            pltpu.VMEM((Z, BOX_DEV, funcs, LANES), F32),
            pltpu.VMEM((Z, BOX_DEV, funcs, LANES), F32),
            pltpu.VMEM((Z, BOX_DEV, LANES), F32),
            pltpu.VMEM((Z, BOX_DEV, LANES), F32),
            pltpu.VMEM((Z, B, 2, funcs, LANES), F32),
            pltpu.VMEM((Z, B, 2, funcs, LANES), F32),
            pltpu.VMEM((B, BOX_DEV, funcs, LANES), F32),
            pltpu.VMEM((B, BOX_DEV, funcs, LANES), F32),
            pltpu.VMEM((B, BOX_DEV, LANES), F32),
            pltpu.VMEM((B, BOX_DEV, LANES), F32),
            dma((15,)),
            dma((blocks,)),
            dma((3,)),
            dma((1 + steps,)),
            dma((1 + steps,)),
            dma((2,)),
            dma((per + 1,)),
            dma((4,)),
            dma((2,)),
            dma((4,)),
        ],
        compiler_params=pltpu.CompilerParams(
            collective_id=0, has_side_effects=True, vmem_limit_bytes=64 * 1024 * 1024
        ),
    )(
        rhs,
        dinv,
        extract.transpose(0, 2, 1),
        lift,
        coef.T,
        nbr.T,
        colour,
        counts,
        send_lo,
        send_hi,
        rec_elem.reshape(1, records),
        rec_owner.T,
        rec_box.reshape(1, records),
        rec_weight.reshape(1, records),
        wall_map,
        fweights,
    )
    return pl.pallas_call(
        hand_over,
        out_shape=(
            jax.ShapeDtypeStruct((BOX_DEV, funcs, LANES), F32),
            jax.ShapeDtypeStruct((BOX_DEV, LANES), F32),
        ),
        in_specs=[hbm] * 2,
        out_specs=(hbm, hbm),
        scratch_shapes=[dma((2,))],
        compiler_params=pltpu.CompilerParams(vmem_limit_bytes=64 * 1024 * 1024),
    )(*sums)


def solution(mesh):
    placed = (
        P("dom", "fn", None),
        P("dom", None, None),
        P(),
        P(),
        P("dom", None),
        P("dom", None),
        P("dom"),
        P("dom"),
        P("dom"),
        P("dom"),
        P("dom"),
        P("dom", None),
        P("dom"),
        P("dom"),
        P(),
        P("fn"),
    )
    return jax.shard_map(
        body,
        mesh=mesh,
        in_specs=placed,
        out_specs=(P("dom", "fn", None), P("dom", None)),
        check_vma=False,
    )
```

```python
import functools
import jax
import jax.numpy as jnp
from jax import lax
from jax.experimental import pallas as pl
from jax.experimental.pallas import tpu as pltpu
from jax.sharding import PartitionSpec as P

BOX_DEV = 4
SWEEPS = 2
OPPOSITE = (1, 0, 3, 2, 5, 4)
LANES = 128
GRIDS = {128: (4, 8, 4), 8: (2, 2, 2)}
MESH = pl.DeviceIdType.MESH
F32 = jnp.float32
BF16 = jnp.bfloat16


def split(value):
    high = value.astype(BF16)
    return high, (value - high.astype(F32)).astype(BF16)


def mm(a, b):
    return jnp.dot(a, b, preferred_element_type=F32)


def far_displacements(X, Y):
    def hops(rd):
        dx, dy = rd // Y, rd % Y
        return min(dx, X - dx) + min(dy, Y - dy)

    longest = 3 if X == 4 else 2
    return [rd for rd in range(X * Y) if hops(rd) == longest]


def hand_over(grad_in, combined_in, grad, combined, sem):
    copies = [
        pltpu.make_async_copy(grad_in, grad, sem.at[0]),
        pltpu.make_async_copy(combined_in, combined, sem.at[1]),
    ]
    for copy in copies:
        copy.start()
    for copy in copies:
        copy.wait()


def kernel(
    dims,
    rhs_hbm,
    dinv_hbm,
    extract_hbm,
    lift_hbm,
    coef_hbm,
    nbr_hbm,
    colour_hbm,
    counts_hbm,
    send_lo_hbm,
    send_hi_hbm,
    rec_elem_hbm,
    rec_owner_hbm,
    rec_box_hbm,
    rec_weight_hbm,
    wall_map_hbm,
    fweights_hbm,
    grad,
    combined,
    rhs,
    dinv,
    extract,
    lift,
    coef,
    nbr,
    colour,
    counts,
    send_lo,
    send_hi,
    rec_elem,
    rec_owner,
    rec_box,
    rec_weight,
    wall_map,
    fweights,
    ext_cat,
    lift_cat,
    psi,
    table,
    scale,
    near_high,
    near_low,
    resid,
    sensed,
    out_up,
    out_down,
    in_below,
    in_above,
    tab_f,
    tab_i,
    sm_f,
    sm_i,
    tabs_in,
    boxes_i,
    sm_boxes,
    send_rec,
    recv_rec,
    z_send,
    z_recv,
    part,
    part_in,
    far_send,
    far_recv,
    last_send,
    last_recv,
    last_part,
    last_part_in,
    load_sem,
    dinv_sem,
    sm_sem,
    up_sem,
    down_sem,
    tab_sem,
    rec_sem,
    z_sem,
    far_sem,
    last_sem,
):
    X, Z, Y = dims
    XY = X * Y
    slots, funcs, width = rhs.shape
    rows = slots * funcs
    trace = extract.shape[1]
    rim = out_up.shape[1]
    records = rec_elem.shape[1]
    owners = X * Z * Y
    chunk = slots // dinv_sem.shape[0]
    me = lax.axis_index("dom")
    fn = lax.axis_index("fn")
    x = me // (Z * Y)
    z = (me // Y) % Z
    y = me % Y
    above = lax.rem(me + 1, owners)
    below = lax.rem(me + owners - 1, owners)

    def place(px, pz, py):
        return (px * Z + pz) * Y + py

    across = [lax.rem(x + dx, X) for dx in range(X)]
    along = [lax.rem(y + dy, Y) for dy in range(Y)]

    def plane_peer(rd):
        return place(across[rd // Y], z, along[rd % Y])

    def wait_for(ref, sem):
        pltpu.make_async_copy(ref, ref, sem).wait()

    def back(rd):
        dx, dy = rd // Y, rd % Y
        return ((X - dx) % X) * Y + (Y - dy) % Y

    far_first = far_displacements(X, Y)
    near_first = [rd for rd in range(XY) if rd not in far_first]
    A, B = len(near_first), len(far_first)

    half = Z // 2
    shifts = [half]
    for step in range(1, half):
        shifts += [half - step, half + step]
    shifts += [0]

    columns = [lax.rem(z + shift, Z) for shift in shifts]

    def column(j):
        return columns[j]

    def opposite(j):
        return shifts.index((Z - shifts[j]) % Z)

    order = (
        (rec_owner_hbm, rec_owner),
        (rec_elem_hbm, rec_elem),
        (rec_box_hbm, rec_box),
        (rec_weight_hbm, rec_weight),
        (colour_hbm, colour),
        (counts_hbm, counts),
        (coef_hbm, coef),
        (nbr_hbm, nbr),
        (send_lo_hbm, send_lo),
        (send_hi_hbm, send_hi),
        (rhs_hbm, rhs),
        (extract_hbm, extract),
        (lift_hbm, lift),
        (wall_map_hbm, wall_map),
        (fweights_hbm, fweights),
    )
    small = []
    for i, (src, dst) in enumerate(order):
        copy = pltpu.make_async_copy(src, dst, load_sem.at[i])
        copy.start()
        small.append(copy)
    chunks = slots // chunk

    def block(i):
        span = pl.ds(i * chunk, chunk)
        return pltpu.make_async_copy(dinv_hbm.at[span], dinv.at[span], dinv_sem.at[i])

    ahead = 3
    for i in range(ahead):
        block(i).start()

    barrier = pltpu.get_barrier_semaphore()
    partners = [(above, fn), (below, fn), (me, 1 - fn)]
    partners += [(plane_peer(rd), fn) for rd in range(1, XY)]
    partners += [(plane_peer(rd), 1 - fn) for rd in far_first]
    partners += [(place(x, column(j), y), fn) for j in range(Z - 1)]
    partners += [(place(x, column(j), y), 1 - fn) for j in range(Z - 1)]
    for partner in partners:
        pl.semaphore_signal(barrier, inc=1, device_id=partner, device_id_type=MESH)

    for copy in small[:4]:
        copy.wait()
    lane = lax.broadcasted_iota(jnp.int32, (records, records), 1)
    sub = lax.broadcasted_iota(jnp.int32, (records, records), 0)
    own = jnp.broadcast_to(rec_owner[...], (records, records)).astype(F32)
    own_col = jnp.sum(jnp.where(lane == sub, own, 0.0), axis=1, keepdims=True)
    same = (own == own_col) & (lane < sub)
    rank = jnp.sum(jnp.where(same, 1.0, 0.0), axis=1, keepdims=True)
    lane_o = lax.broadcasted_iota(jnp.int32, (records, owners), 1).astype(F32)
    first = jnp.where((own_col == lane_o) & (rank < 0.5), 1.0, 0.0)
    second = jnp.where((own_col == lane_o) & (rank > 0.5), 1.0, 0.0)
    row = lax.broadcasted_iota(jnp.int32, (8, records), 0)
    elem_b = jnp.broadcast_to(rec_elem[...].astype(F32), (8, records))
    box_b = jnp.broadcast_to(rec_box[...].astype(F32), (8, records))
    weight_b = jnp.broadcast_to(rec_weight[...], (8, records))

    def rows_at(s):
        return jnp.where(
            row == s, box_b, jnp.where(row == 2 + s, elem_b, jnp.where(row == 4 + s, weight_b, 0.0))
        )

    tab = jnp.dot(
        rows_at(0), first, precision=lax.Precision.HIGHEST, preferred_element_type=F32
    ) + jnp.dot(
        rows_at(1), second, precision=lax.Precision.HIGHEST, preferred_element_type=F32
    )
    tab_f[...] = tab
    tab_i[...] = jnp.clip((tab + 0.25).astype(jnp.int32), 0, slots - 1)
    to_smem = [
        pltpu.make_async_copy(tab_f, sm_f, sm_sem.at[0]),
        pltpu.make_async_copy(tab_i, sm_i, sm_sem.at[1]),
    ]
    for copy in to_smem:
        copy.start()

    full = width // (2 * LANES) * 2 * LANES
    table[:, 0] = jnp.zeros((6, funcs, LANES), F32)
    small[11].wait()
    small[12].wait()
    for f in range(6):
        pad = jnp.zeros((LANES - trace, width), F32)
        value = jnp.concatenate([extract[OPPOSITE[f]], pad], axis=0)
        high, low = split(value.T)
        cols = slice(f * LANES, (f + 1) * LANES)
        pieces = [high[:full], high[:full], low[:full], high[full:], high[full:], low[full:]]
        if 3 * width < ext_cat.shape[0]:
            pieces += [jnp.zeros((ext_cat.shape[0] - 3 * width, LANES), BF16)]
        ext_cat[:, cols] = jnp.concatenate(pieces, axis=0)
        pad = jnp.zeros((LANES - trace, width), F32)
        high, low = split(jnp.concatenate([lift[f], pad], axis=0))
        lift_cat[0, f * LANES : (f + 1) * LANES] = high
        lift_cat[1, f * LANES : (f + 1) * LANES] = low

    small[6].wait()

    def spread(i, _):
        for k in range(8):
            for f in range(6):
                scale[f, i * 8 + k] = jnp.full((funcs, LANES), coef[f, i * 8 + k], F32)
        return 0

    lax.fori_loop(0, slots // 8, spread, 0)
    small[4].wait()
    small[5].wait()
    live = counts[0]
    batch = slots

    def chosen(e, shade):
        mask = jnp.where((colour[e] == shade) & (e < live), 1, 0)
        return jnp.full((funcs, width), mask, jnp.int32) > 0

    def update(first_e, count, shade, source, first_step):
        fresh = []
        for k in range(count):
            value = source(first_e + k).astype(BF16)
            fresh.append(mm(value, dinv[first_e + k]))
        for k in range(count):
            e = first_e + k
            old = jnp.zeros((funcs, width), F32) if first_step else psi[e]
            psi[e] = jnp.where(chosen(e, shade), fresh[k], old)

    def terms(value):
        high, low = split(value)
        pieces = [high[:, :full], low[:, :full], high[:, :full]]
        pieces += [high[:, full:], low[:, full:], high[:, full:]]
        if 3 * width < ext_cat.shape[0]:
            pieces += [jnp.zeros((value.shape[0], ext_cat.shape[0] - 3 * width), BF16)]
        return jnp.concatenate(pieces, axis=1)

    def fill(first_e, count):
        span = pl.ds(first_e, count)
        out = mm(terms(psi[span].reshape(count * funcs, width)), ext_cat[...])
        for f in range(6):
            table[f, pl.ds(first_e + 1, count)] = out[:, f * LANES : (f + 1) * LANES].reshape(
                count, funcs, LANES
            )

    small[10].wait()

    def start(i, _):
        block(i).wait()

        @pl.when(i + ahead < chunks)
        def _():
            block(i + ahead).start()

        update(i * chunk, chunk, 0, lambda e: rhs[e], True)
        return 0

    lax.fori_loop(0, chunks, start, 0)
    for i in (7, 8, 9, 13, 14):
        small[i].wait()
    pl.semaphore_wait(barrier, len(partners))
    def chain(index):
        up = pltpu.make_async_remote_copy(
            src_ref=out_up.at[index],
            dst_ref=in_below.at[index],
            send_sem=up_sem.at[0],
            recv_sem=up_sem.at[1 + index],
            device_id=(above, fn),
            device_id_type=MESH,
        )
        down = pltpu.make_async_remote_copy(
            src_ref=out_down.at[index],
            dst_ref=in_above.at[index],
            send_sem=down_sem.at[0],
            recv_sem=down_sem.at[1 + index],
            device_id=(below, fn),
            device_id_type=MESH,
        )
        return up, down

    def export(index, away):
        out = mm(terms(jnp.concatenate(away, axis=0)), ext_cat[:, : 2 * LANES])
        count = rim * funcs
        out_up[index] = out[:count, :LANES].reshape(rim, funcs, LANES)
        out_down[index] = out[count:, LANES:].reshape(rim, funcs, LANES)
        for copy in chain(index):
            copy.start()

    listed = [send_hi[s] for s in range(rim)] + [send_lo[s] for s in range(rim)]
    export(0, [psi[e] for e in listed])

    def step_body(step, _):
        shade = lax.rem(step, 2)

        @pl.when(step == 2)
        def _():
            homes = [
                (plane_peer(rd), near_first.index(back(rd))) for rd in near_first[1:]
            ]
            homes += [(place(x, column(j), y), A + opposite(j)) for j in range(Z - 1)]
            for peer, home in homes:
                pltpu.make_async_remote_copy(
                    src_ref=tab_f,
                    dst_ref=tabs_in.at[home],
                    send_sem=tab_sem.at[0],
                    recv_sem=tab_sem.at[1],
                    device_id=(peer, fn),
                    device_id_type=MESH,
                ).start()

        @pl.when(step > 0)
        def _():
            fill(0, slots)

        def gather(faces):
            def pairs(i, _):
                for f in faces:
                    found = []
                    for k in range(4):
                        e = i * 8 + k * 2
                        found.append(
                            jnp.concatenate(
                                [
                                    table[f, nbr[f, e] + 1] * scale[f, e],
                                    table[f, nbr[f, e + 1] + 1] * scale[f, e + 1],
                                ],
                                axis=0,
                            )
                        )
                    found = [split(value) for value in found]
                    for k in range(4):
                        start = pl.multiple_of((i * 8 + k * 2) * funcs, 2 * funcs)
                        at = pl.ds(start, 2 * funcs)
                        near_high[at, f * LANES : (f + 1) * LANES] = found[k][0]
                        near_low[at, f * LANES : (f + 1) * LANES] = found[k][1]
                return 0

            lax.fori_loop(0, slots // 8, pairs, 0)

        def lifted(lo, hi):
            a, b = lo * LANES, hi * LANES
            left = jnp.concatenate([near_high[:, a:b], near_low[:, a:b], near_high[:, a:b]], axis=1)
            right = jnp.concatenate([lift_cat[0, a:b], lift_cat[0, a:b], lift_cat[1, a:b]], axis=0)
            return mm(left, right)

        gather((2, 3, 4, 5))
        resid[...] = rhs[...] - lifted(2, 6).reshape(slots, funcs, width)
        for copy in chain(step - 1):
            copy.wait_recv()
        table[0, slots + 1 : slots + 1 + rim] = in_below[step - 1]
        table[1, slots + 1 + rim : slots + 1 + 2 * rim] = in_above[step - 1]
        gather((0, 1))
        resid[...] = resid[...] - lifted(0, 2).reshape(slots, funcs, width)

        @pl.when(step < 2 * SWEEPS - 1)
        def _():
            fresh = [mm(resid[e].astype(BF16), dinv[e]) for e in listed]
            export(
                step, [jnp.where(chosen(e, shade), new, psi[e]) for e, new in zip(listed, fresh)]
            )

        def sweep(i, _):
            update(i * batch, batch, shade, lambda e: resid[e], False)
            return 0

        lax.fori_loop(0, slots // batch, sweep, 0)
        return 0

    lax.fori_loop(1, 2 * SWEEPS, step_body, 0)

    high, low = split(psi[...].reshape(rows, width))
    sensed[...] = (mm(high, wall_map[...]) + mm(low, wall_map[...])).reshape(
        slots, funcs, LANES
    )
    for copy in to_smem:
        copy.wait()

    def slot(owner, which):
        return sensed[sm_i[2 + which, owner]] * sm_f[4 + which, owner]

    for j in range(Z):
        for d, rd in enumerate(far_first):
            px, py = across[rd // Y], along[rd % Y]
            for which in range(2):
                far_send[j, d, which] = slot(place(px, column(j), py), which)
    for j in range(Z):
        if j < Z - 1:
            pltpu.make_async_remote_copy(
                src_ref=far_send.at[j],
                dst_ref=far_recv.at[opposite(j)],
                send_sem=far_sem.at[0],
                recv_sem=far_sem.at[1],
                device_id=(place(x, column(j), y), fn),
                device_id_type=MESH,
            ).start()
    per = rec_sem.shape[0] - 1
    group = Z // per

    def send_near(c):
        span = pl.ds(c * group, group)
        for a, rd in enumerate(near_first):
            px, py = across[rd // Y], along[rd % Y]
            for j in range(c * group, (c + 1) * group):
                for which in range(2):
                    send_rec[a, j, which] = slot(place(px, column(j), py), which)
        for a, rd in enumerate(near_first):
            if a:
                pltpu.make_async_remote_copy(
                    src_ref=send_rec.at[a, span],
                    dst_ref=recv_rec.at[near_first.index(back(rd)), span],
                    send_sem=rec_sem.at[per],
                    recv_sem=rec_sem.at[c],
                    device_id=(plane_peer(rd), fn),
                    device_id_type=MESH,
                ).start()

    for c in range(per):
        send_near(c)
    wait_for(tabs_in.at[1 : A + Z - 1], tab_sem.at[1])
    tabs_in[0] = tab_f[...]
    tabs_in[A + Z - 1] = tab_f[...]
    boxes_i[...] = (tabs_in[...] + 0.25).astype(jnp.int32)
    boxes = pltpu.make_async_copy(boxes_i, sm_boxes, sm_sem.at[2])
    boxes.start()
    boxes.wait()

    sub_f = lax.broadcasted_iota(jnp.int32, (funcs, LANES), 0)
    weight = jnp.zeros((funcs, LANES), F32)
    for j in range(funcs):
        weight = jnp.where(sub_f == j, fweights[j], weight)
    none = (jnp.zeros((funcs, LANES), F32),) * BOX_DEV

    def add(value, box, total):
        which = jnp.full((funcs, LANES), box, jnp.int32)
        return tuple(t + jnp.where(which == b, value, 0.0) for b, t in enumerate(total))

    def weighted(total):
        return jnp.concatenate(
            [jnp.sum(total[b] * weight, axis=0, keepdims=True) for b in range(BOX_DEV)], axis=0
        )

    def hand_on(total, full, summed, at, full_in, summed_in, home, peer, sems):
        for b in range(BOX_DEV):
            full[at, b] = total[b]
        pltpu.make_async_remote_copy(
            src_ref=full.at[at],
            dst_ref=full_in.at[home],
            send_sem=sems.at[0],
            recv_sem=sems.at[1],
            device_id=(peer, fn),
            device_id_type=MESH,
        ).start()
        summed[at] = weighted(total)
        pltpu.make_async_remote_copy(
            src_ref=summed.at[at],
            dst_ref=summed_in.at[home],
            send_sem=sems.at[2],
            recv_sem=sems.at[3],
            device_id=(peer, 1 - fn),
            device_id_type=MESH,
        ).start()

    def near_sums(c):
        wait_for(recv_rec.at[1:, pl.ds(c * group, group)], rec_sem.at[c])
        for j in range(c * group, (c + 1) * group):
            owner = place(x, column(j), y)
            total = none
            for s in range(2):
                total = add(send_rec[0, j, s], sm_boxes[0, s, owner], total)

            def accumulate(a, total):
                for s in range(2):
                    total = add(recv_rec[a, j, s], sm_boxes[a, s, owner], total)
                return total

            total = lax.fori_loop(1, A, accumulate, total)
            if j < Z - 1:
                peer = place(x, column(j), y)
                hand_on(total, z_send, part, j, z_recv, part_in, opposite(j), peer, z_sem)
            else:
                for b in range(BOX_DEV):
                    z_send[j, b] = total[b]
                part[j] = weighted(total)
                pltpu.make_async_remote_copy(
                    src_ref=part.at[j],
                    dst_ref=part_in.at[j],
                    send_sem=z_sem.at[2],
                    recv_sem=z_sem.at[3],
                    device_id=(me, 1 - fn),
                    device_id_type=MESH,
                ).start()

    def far_sums():
        wait_for(far_recv.at[: Z - 1], far_sem.at[1])
        for d, rd in enumerate(far_first):
            px, py = across[rd // Y], along[rd % Y]
            owner = place(px, z, py)
            total = none
            for s in range(2):
                total = add(far_send[Z - 1, d, s], sm_boxes[A + Z - 1, s, owner], total)

            def accumulate(j, total):
                for s in range(2):
                    total = add(far_recv[j, d, s], sm_boxes[A + j, s, owner], total)
                return total

            total = lax.fori_loop(0, Z - 1, accumulate, total)
            home = far_first.index(back(rd))
            hand_on(
                total, last_send, last_part, d, last_recv, last_part_in, home, owner, last_sem
            )

    for c in range(per):
        near_sums(c)
        if c == 0:
            far_sums()

    result = z_send[Z - 1]
    wait_for(z_recv.at[: Z - 1], z_sem.at[1])
    wait_for(part_in, z_sem.at[3])
    own_part = part_in[Z - 1]
    for j in range(Z - 1):
        result = result + z_recv[j]
        own_part = own_part + part_in[j]
    wait_for(last_recv, last_sem.at[1])
    wait_for(last_part_in, last_sem.at[3])
    for d in range(B):
        result = result + last_recv[d]
        own_part = own_part + last_part_in[d]
    grad[...] = result
    combined[...] = own_part + jnp.sum(result * weight[None], axis=1)

    wait_for(out_up, up_sem.at[0])
    wait_for(out_down, down_sem.at[0])
    wait_for(tabs_in.at[1 : A + Z - 1], tab_sem.at[0])
    wait_for(send_rec.at[1:], rec_sem.at[per])
    wait_for(z_send.at[: Z - 1], z_sem.at[0])
    wait_for(part, z_sem.at[2])
    wait_for(far_send.at[: Z - 1], far_sem.at[0])
    wait_for(last_send, last_sem.at[0])
    wait_for(last_part, last_sem.at[2])


def body(
    rhs,
    dinv,
    extract,
    lift,
    coef,
    nbr,
    colour,
    counts,
    send_lo,
    send_hi,
    rec_elem,
    rec_owner,
    rec_box,
    rec_weight,
    wall_map,
    fweights,
):
    slots, funcs, width = rhs.shape
    rim = send_lo.shape[0]
    records = rec_elem.shape[0]
    owners = lax.axis_size("dom")
    X, Z, Y = GRIDS[owners]
    rows = slots * funcs
    steps = 2 * SWEEPS - 1
    blocks = 8
    per = min(4, Z)
    B = len(far_displacements(X, Y))
    A = X * Y - B
    hbm = pl.BlockSpec(memory_space=pltpu.HBM)
    vmem = pl.BlockSpec(memory_space=pltpu.VMEM)
    dma = pltpu.SemaphoreType.DMA
    sums = pl.pallas_call(
        functools.partial(kernel, (X, Z, Y)),
        out_shape=(
            jax.ShapeDtypeStruct((BOX_DEV, funcs, LANES), F32),
            jax.ShapeDtypeStruct((BOX_DEV, LANES), F32),
        ),
        in_specs=[hbm] * 16,
        out_specs=(vmem, vmem),
        scratch_shapes=[
            pltpu.VMEM(rhs.shape, F32),
            pltpu.VMEM(dinv.shape, BF16),
            pltpu.VMEM(lift.shape, F32),
            pltpu.VMEM(lift.shape, F32),
            pltpu.SMEM((6, slots), F32),
            pltpu.SMEM((6, slots), jnp.int32),
            pltpu.SMEM((slots,), jnp.int32),
            pltpu.SMEM((1,), jnp.int32),
            pltpu.SMEM((rim,), jnp.int32),
            pltpu.SMEM((rim,), jnp.int32),
            pltpu.VMEM((1, records), jnp.int32),
            pltpu.VMEM((1, records), jnp.int32),
            pltpu.VMEM((1, records), jnp.int32),
            pltpu.VMEM((1, records), F32),
            pltpu.VMEM(wall_map.shape, BF16),
            pltpu.SMEM((funcs,), F32),
            pltpu.VMEM((pl.cdiv(3 * width, 2 * LANES) * 2 * LANES, 6 * LANES), BF16),
            pltpu.VMEM((2, 6 * LANES, width), BF16),
            pltpu.VMEM((slots, funcs, width), F32),
            pltpu.VMEM((6, slots + 2 * rim + 1, funcs, LANES), F32),
            pltpu.VMEM((6, slots, funcs, LANES), F32),
            pltpu.VMEM((rows, 6 * LANES), BF16),
            pltpu.VMEM((rows, 6 * LANES), BF16),
            pltpu.VMEM((slots, funcs, width), F32),
            pltpu.VMEM((slots, funcs, LANES), F32),
            pltpu.VMEM((steps, rim, funcs, LANES), F32),
            pltpu.VMEM((steps, rim, funcs, LANES), F32),
            pltpu.VMEM((steps, rim, funcs, LANES), F32),
            pltpu.VMEM((steps, rim, funcs, LANES), F32),
            pltpu.VMEM((8, owners), F32),
            pltpu.VMEM((8, owners), jnp.int32),
            pltpu.SMEM((8, owners), F32),
            pltpu.SMEM((8, owners), jnp.int32),
            pltpu.VMEM((A + Z, 8, owners), F32),
            pltpu.VMEM((A + Z, 8, owners), jnp.int32),
            pltpu.SMEM((A + Z, 8, owners), jnp.int32),
            pltpu.VMEM((A, Z, 2, funcs, LANES), F32),
            pltpu.VMEM((A, Z, 2, funcs, LANES), F32),
            pltpu.VMEM((Z, BOX_DEV, funcs, LANES), F32),
            pltpu.VMEM((Z, BOX_DEV, funcs, LANES), F32),
            pltpu.VMEM((Z, BOX_DEV, LANES), F32),
            pltpu.VMEM((Z, BOX_DEV, LANES), F32),
            pltpu.VMEM((Z, B, 2, funcs, LANES), F32),
            pltpu.VMEM((Z, B, 2, funcs, LANES), F32),
            pltpu.VMEM((B, BOX_DEV, funcs, LANES), F32),
            pltpu.VMEM((B, BOX_DEV, funcs, LANES), F32),
            pltpu.VMEM((B, BOX_DEV, LANES), F32),
            pltpu.VMEM((B, BOX_DEV, LANES), F32),
            dma((15,)),
            dma((blocks,)),
            dma((3,)),
            dma((1 + steps,)),
            dma((1 + steps,)),
            dma((2,)),
            dma((per + 1,)),
            dma((4,)),
            dma((2,)),
            dma((4,)),
        ],
        compiler_params=pltpu.CompilerParams(
            collective_id=0, has_side_effects=True, vmem_limit_bytes=64 * 1024 * 1024
        ),
    )(
        rhs,
        dinv,
        extract.transpose(0, 2, 1),
        lift,
        coef.T,
        nbr.T,
        colour,
        counts,
        send_lo,
        send_hi,
        rec_elem.reshape(1, records),
        rec_owner.T,
        rec_box.reshape(1, records),
        rec_weight.reshape(1, records),
        wall_map,
        fweights,
    )
    return pl.pallas_call(
        hand_over,
        out_shape=(
            jax.ShapeDtypeStruct((BOX_DEV, funcs, LANES), F32),
            jax.ShapeDtypeStruct((BOX_DEV, LANES), F32),
        ),
        in_specs=[hbm] * 2,
        out_specs=(hbm, hbm),
        scratch_shapes=[dma((2,))],
        compiler_params=pltpu.CompilerParams(vmem_limit_bytes=64 * 1024 * 1024),
    )(*sums)


def solution(mesh):
    placed = (
        P("dom", "fn", None),
        P("dom", None, None),
        P(),
        P(),
        P("dom", None),
        P("dom", None),
        P("dom"),
        P("dom"),
        P("dom"),
        P("dom"),
        P("dom"),
        P("dom", None),
        P("dom"),
        P("dom"),
        P(),
        P("fn"),
    )
    return jax.shard_map(
        body,
        mesh=mesh,
        in_specs=placed,
        out_specs=(P("dom", "fn", None), P("dom", None)),
        check_vma=False,
    )
```
